256 devices in a mesh: dp: 128 (over z, y, x), ep: 2 (over core).
Axes of the slice: x: 4, y: 4, z: 8, core: 2. Of those that a mesh axis runs over, the one named last changes fastest.
Arguments:
- queries: bfloat16 [2048, 64, 576], P('dp'), may hold values from -65 to 65
- latent_cache: bfloat16 [2048, 256, 576], P('dp', 'ep'), may hold values from -6 to 6
- cache_lens: int32 [2048], P('dp'), may hold values from 2 to 256
- movers: int32 [128, 4], P('dp'), may hold values from 0 to 16, as said below
- hidden: bfloat16 [2048, 7168], P('dp'), may hold values from -6 to 6
- norm_gain: float32 [7168], replicated, may hold values from 0.1 to 1.9
- routes: int32 [2048, 8], P('dp'), may hold values from 0 to 31, all different within a row; in each aligned block of 16 rows (0 to 15, 16 to 31, ...) at most 8 rows name the same one
- gate_weights: bfloat16 [2048, 8], P('dp'), may hold values from 0.19921875 to 1
- gate_proj: bfloat16 [128, 7168, 256], P('dp', None, 'ep'), may hold values from -0.0625 to 0.0625
- up_proj: bfloat16 [128, 7168, 256], P('dp', None, 'ep'), may hold values from -0.0625 to 0.0625
- down_proj: bfloat16 [128, 1024, 1792], P('dp', None, 'ep'), may hold values from -0.1875 to 0.1875
Outputs:
- served: bfloat16 [2560, 64, 512], P('dp', 'ep')
- expert_mix: bfloat16 [2048, 7168], P('dp', 'ep')
The draws below stay inside these ranges and needn't reach their ends.
Inputs may be any that keep to these rules, and one draw needn't show every extreme that they name: `movers`: row i lists distinct request slots of rank i, followed by 16 in unused entries; a rank whose partner (i + 64) mod 128 lists any slot lists none itself. `routes`: each row names 8 different experts; among the 16 rows of one dp rank no expert is named more than 8 times.
All inputs are finite; a program needn't handle non-finite values.
Results may differ from the reference program's by a relative error of at most 0.015.
Values may be sent and summed in bfloat16 or wider, within the bound.
No kernel may reach another device: no remote copies, remote signals or barrier semaphores. Data moves between devices by JAX's collectives and lax.ppermute only.
A program may use at most 128 MiB of HBM per device.

```python
import math
import jax
import jax.numpy as jnp
import numpy as np
from jax import lax

D = 7168
HEADS = 64
LAT = 512
KD = 576
HID = 1024
TOP = 8
REQ = 16
L_MAX = 256
MIG = 4
EXPERTS = 32
GROUP = 4
CAP = 8
SLOTS = 20
TOTAL_REQ = 2048
N_DP = 128
N_EP = 2


def request_plan(key):
    heavy_key, length_key, pick_key, count_key = jax.random.split(jax.random.fold_in(key, 7), 4)
    is_heavy = jax.random.randint(heavy_key, (N_DP,), 0, 2)
    is_heavy = is_heavy.at[N_DP // 2].set(1).at[0].set(0)
    long_lens = jax.random.randint(length_key, (N_DP, REQ), L_MAX // 2, L_MAX + 1)
    short_lens = jax.random.randint(jax.random.fold_in(length_key, 1), (N_DP, REQ), 2, L_MAX // 4 + 1)
    lengths = jnp.where(is_heavy[:, None] == 1, long_lens, short_lens)
    lengths = lengths.at[N_DP // 2, 0].set(L_MAX)
    partner = jnp.roll(is_heavy, -(N_DP // 2))
    moving = (is_heavy == 1) & (partner == 0)
    counts = jax.random.randint(count_key, (N_DP,), 1, MIG + 1)
    counts = counts.at[N_DP // 2].set(MIG)
    counts = jnp.where(moving, counts, 0)
    scores = jax.random.randint(pick_key, (N_DP, REQ), 0, 1 << 20) * REQ + jnp.arange(REQ)[None, :]
    ranking = jnp.argsort(scores, axis=1)[:, :MIG]
    listed = jnp.where(jnp.arange(MIG)[None, :] < counts[:, None], ranking, REQ)
    return (lengths.reshape(-1).astype(jnp.int32), listed.astype(jnp.int32))


def draw_cache_lens(key, part):
    lengths, listed = request_plan(key)
    return lengths


def draw_movers(key, part):
    lengths, listed = request_plan(key)
    return listed


def draw_latent_cache(key, part):
    key = jax.random.fold_in(key, 1)
    values = jnp.clip(jax.random.normal(key, (TOTAL_REQ, L_MAX, KD), jnp.float32), -6.0, 6.0)
    return values.astype(jnp.bfloat16)


def draw_queries(key, part):
    key = jax.random.fold_in(key, 2)
    values = jnp.clip(jax.random.normal(key, (TOTAL_REQ, HEADS, KD), jnp.float32), -6.0, 6.0)
    return values.astype(jnp.bfloat16)


def block_scale(stream_key, shape, pieces, smallest, high):
    def one(position, shards_of):
        draws = jax.random.uniform(jax.random.fold_in(jax.random.fold_in(stream_key, 6), position), (shards_of,), jnp.float32, smallest / len(pieces), high / len(pieces))
        return jnp.repeat(jnp.exp(draws), shape[position] // shards_of).reshape((-1,) + (1,) * (len(shape) - position - 1))

    level = one(*pieces[0])
    for cut in pieces[1:]:
        level = level * one(*cut)
    return level


def routed_block(rng, own, number, rows, amount, top, limit, skew):
    order = jax.random.permutation(rng, amount)
    packed, common = load_shares(amount, rows * top, limit, skew, True), load_shares(amount, rows * top, limit, skew, False)
    places = jnp.arange(amount)

    def named(tallies, rotation):
        used = int((tallies > 0).sum())
        fixed = max(1, used // 4)
        shifted = fixed + (places - fixed + rotation * (used - fixed)) % max(1, amount - fixed)
        return jnp.zeros((amount,), jnp.int32).at[order[jnp.where(places < fixed, places, shifted)]].set(jnp.asarray(tallies, jnp.int32))

    tallies = jnp.where(number % 4 == 0, named(packed, number // 4), named(common, number - number // 4 - 1))
    mixed = jax.random.permutation(jax.random.fold_in(own, 3), amount)
    source_of, taker = mixed[0:amount // 2 * 2:2], mixed[1:amount // 2 * 2:2]
    room = jnp.minimum(tallies[source_of] - 1, limit - tallies[taker]) // 2
    room = jnp.where((source_of == order[0]) | (taker == order[0]) | (tallies[taker] == 0), 0, jnp.maximum(room, 0))
    shifted = jax.random.randint(jax.random.fold_in(own, 4), (amount // 2,), 0, 1 << 20) % (room + 1)
    tallies = tallies.at[source_of].add(-shifted).at[taker].add(shifted)
    labels = jnp.searchsorted(jnp.cumsum(tallies), jnp.arange(rows * top), side="right").astype(jnp.int32)
    listing = labels.reshape(top, rows).T
    listing = listing[jax.random.permutation(jax.random.fold_in(own, 1), rows)]
    rotation = jax.random.randint(jax.random.fold_in(own, 2), (rows, 1), 0, top)
    return jnp.take_along_axis(listing, (jnp.arange(top)[None, :] + rotation) % top, axis=1)


def load_shares(number_of, total, bound, skew, full):
    portions = [(1 << 20) // math.isqrt(standing ** skew) + 1 for standing in range(1, number_of + 1)]
    largest = bound if full else min(bound, max(-(-total // number_of), total * portions[0] // sum(portions)))
    least = 1 if total - largest >= number_of - 1 else 0
    given, spare = [largest] + [least] * (number_of - 1), total - largest - least * (number_of - 1)
    while spare > 0:
        candidates = [i for i in range(1, number_of) if given[i] < largest] or [i for i in range(1, number_of) if given[i] < bound]
        pool, left = sum([portions[i] for i in candidates]), spare
        for i in candidates:
            extra = min(bound - given[i], max(1, left * portions[i] // pool), spare)
            given[i] = given[i] + extra
            spare = spare - extra
    return np.array(given)


def normal_values(own_key, shape, deviation, most, cuts=(), kind=jnp.bfloat16):
    entries = deviation * jax.random.normal(own_key, shape, jnp.float32)
    if cuts:
        entries = entries * block_scale(own_key, shape, cuts, -0.22, 0.18)
    return jnp.clip(entries, -most, most).astype(kind)


def setup_inputs(seed: int = 0) -> dict:
    splits = jax.random.split(jax.random.key(seed), 12)
    queries = draw_queries(jax.random.fold_in(splits[11], 71), 0)
    latent_cache = draw_latent_cache(jax.random.fold_in(splits[11], 71), 0)
    cache_lens = draw_cache_lens(jax.random.fold_in(splits[11], 71), 0)
    movers = draw_movers(jax.random.fold_in(splits[11], 71), 0)
    hidden = normal_values(splits[4], (TOTAL_REQ, D), 1.0, 6.0, ((0, 128),))
    norm_gain = jnp.clip(1.0 + 0.18 * jax.random.normal(splits[5], (D,), jnp.float32), 0.1, 1.9)
    routes_keys = jax.random.split(jax.random.fold_in(splits[6], 1), TOTAL_REQ // REQ)
    routes_turns = jax.random.permutation(jax.random.fold_in(splits[6], 3), TOTAL_REQ // REQ)
    routes = jax.vmap(lambda own, number: routed_block(jax.random.fold_in(splits[6], 2), own, number, REQ, EXPERTS, TOP, CAP, 2))(routes_keys, routes_turns).reshape((TOTAL_REQ, TOP))
    gate_weights = jnp.clip(0.19921875 + 0.80078125 * jax.random.uniform(splits[7], (TOTAL_REQ, TOP), jnp.float32) ** block_scale(splits[7], (TOTAL_REQ, TOP), ((0, 128),), -0.2, 0.2), 0.19921875, 1.0).astype(jnp.bfloat16)
    gate_proj = normal_values(splits[8], (N_DP, D, HID // GROUP), D ** -0.5, 0.0625, ((0, 128), (2, 2)))
    up_proj = normal_values(splits[9], (N_DP, D, HID // GROUP), D ** -0.5, 0.0625, ((0, 128), (2, 2)))
    down_proj = normal_values(splits[10], (N_DP, HID, D // GROUP), HID ** -0.5, 0.1875, ((0, 128), (2, 2)))
    return {"queries": queries, "latent_cache": latent_cache, "cache_lens": cache_lens, "movers": movers, "hidden": hidden, "norm_gain": norm_gain, "routes": routes, "gate_weights": gate_weights, "gate_proj": gate_proj, "up_proj": up_proj, "down_proj": down_proj}


softmax_scale = 192 ** (-0.5)

def rank_attention(operands):
    queries, latent_cache, lengths = operands
    scores = jnp.einsum('rhc,rtc->rht', queries.astype(jnp.float32), latent_cache.astype(jnp.float32)) * softmax_scale
    positions = jnp.arange(latent_cache.shape[1], dtype=jnp.int32)
    is_valid = positions[None, None, :] < lengths[:, None, None]
    masked = jnp.where(is_valid, scores, -1e+30)
    row_peak = lax.optimization_barrier(jnp.max(masked, axis=2, keepdims=True))
    weights = jnp.where(is_valid, jnp.exp(masked - row_peak), 0.0)
    denominator = lax.optimization_barrier(jnp.sum(weights, axis=2))
    lowered = lax.optimization_barrier(weights.astype(jnp.bfloat16))
    rounded = lowered.astype(jnp.float32)
    numerator = jnp.einsum('rht,rtc->rhc', rounded, latent_cache[:, :, :LAT].astype(jnp.float32))
    return (numerator / denominator[:, :, None]).astype(jnp.bfloat16)

def pick_rows(context_rank, indices):
    return context_rank[indices]

def reference(queries, latent_cache, cache_lens, movers, hidden, norm_gain, routes, gate_weights, gate_proj, up_proj, down_proj):
    context = lax.map(rank_attention, (queries.reshape(N_DP, REQ, HEADS, KD), latent_cache.reshape(N_DP, REQ, L_MAX, KD), cache_lens.reshape(N_DP, REQ)))
    slot_ids = jnp.arange(REQ, dtype=jnp.int32)
    flagged = jnp.any(slot_ids[None, :, None] == movers[:, None, :], axis=2)
    nothing = jnp.zeros((), jnp.bfloat16)
    own_part = jnp.where(flagged[:, :, None, None], nothing, context)
    partner_context = jnp.roll(context, -(N_DP // 2), axis=0)
    partner_movers = jnp.roll(movers, -(N_DP // 2), axis=0)
    picked = jax.vmap(pick_rows)(partner_context, jnp.minimum(partner_movers, REQ - 1).astype(jnp.int32))
    moved_part = jnp.where((partner_movers < REQ)[:, :, None, None], picked, nothing)
    served = jnp.concatenate([own_part, moved_part], axis=1).reshape(N_DP * SLOTS, HEADS, LAT)
    widened = hidden.astype(jnp.float32)
    normed = (widened * lax.rsqrt(lax.optimization_barrier(jnp.mean(widened * widened, axis=1, keepdims=True)) + 1e-06) * norm_gain).astype(jnp.bfloat16)
    per_rank = routes.reshape(N_DP, REQ * TOP)
    onehot = (per_rank[:, :, None] == jnp.arange(EXPERTS, dtype=jnp.int32)[None, None, :]).astype(jnp.int32)
    earlier = jnp.cumsum(onehot, axis=1) - onehot
    slot_index = lax.optimization_barrier(jnp.sum(earlier * onehot, axis=2))
    column = jnp.arange(N_DP, dtype=jnp.int32)[:, None] * CAP + slot_index
    row_index = jnp.broadcast_to(jnp.arange(TOTAL_REQ, dtype=jnp.int32).reshape(N_DP, REQ, 1), (N_DP, REQ, TOP)).reshape(N_DP, REQ * TOP)
    row_table = jnp.full((EXPERTS, N_DP * CAP), TOTAL_REQ, jnp.int32).at[per_rank, column].set(row_index)
    gate_table = jnp.zeros((EXPERTS, N_DP * CAP), jnp.float32).at[per_rank, column].set(gate_weights.reshape(N_DP, REQ * TOP).astype(jnp.float32))
    padded = jnp.concatenate([normed, jnp.zeros((1, D), jnp.bfloat16)], axis=0)
    gate_blocks = gate_proj.reshape(EXPERTS, GROUP, D, HID // GROUP)
    up_blocks = up_proj.reshape(EXPERTS, GROUP, D, HID // GROUP)
    down_blocks = down_proj.reshape(EXPERTS, GROUP, HID, N_EP, D // (GROUP * N_EP))

    def expert_step(running, operands):
        row_ids, gate_values, gate_block, up_block, down_block = operands
        gate_matrix = jnp.transpose(gate_block, (1, 0, 2)).reshape(D, HID)
        up_matrix = jnp.transpose(up_block, (1, 0, 2)).reshape(D, HID)
        down_matrix = jnp.transpose(down_block, (1, 2, 0, 3)).reshape(HID, D)
        chosen = padded[row_ids]
        gate_val = jnp.dot(chosen, gate_matrix, preferred_element_type=jnp.float32)
        up_val = jnp.dot(chosen, up_matrix, preferred_element_type=jnp.float32)
        activated = (jax.nn.silu(gate_val) * up_val).astype(jnp.bfloat16)
        expert_out = jnp.dot(activated, down_matrix, preferred_element_type=jnp.float32).astype(jnp.bfloat16)
        running = running.at[row_ids].add(gate_values[:, None] * expert_out.astype(jnp.float32))
        return (running, None)
    summed, _ = lax.scan(expert_step, jnp.zeros((TOTAL_REQ + 1, D), jnp.float32), (row_table, gate_table, gate_blocks, up_blocks, down_blocks))
    expert_mix = (widened + summed[:TOTAL_REQ]).astype(jnp.bfloat16)
    return (served, expert_mix)
```

```python
import jax
import jax.numpy as jnp
from jax import lax
from jax.sharding import Mesh, PartitionSpec as P

LAT = 512
EXPERTS = 32
CAP = 8
PLANE = ("z", "y")
SOFTMAX_SCALE = 192 ** (-0.5)
CHUNKS = 2
BF = jnp.bfloat16
F32 = jnp.float32


def shifted(x, axis, by):
    devices = lax.axis_size(axis)
    return lax.ppermute(x, axis, [(i, (i + by) % devices) for i in range(devices)])


def attend(queries, latent_cache, lengths, core):
    span = latent_cache.shape[1]
    heads = queries.shape[1] // 2
    scores = jnp.einsum("shc,stc->sht", queries, latent_cache, preferred_element_type=F32)
    scores = scores * SOFTMAX_SCALE
    positions = core * span + jnp.arange(span, dtype=jnp.int32)
    valid = positions[None, None, :] < lengths[:, None, None]
    masked = jnp.where(valid, scores, -1e30)
    peak = jnp.max(masked, axis=2)
    weights = jnp.where(valid, jnp.exp(masked - peak[:, :, None]), 0.0)
    total = jnp.sum(weights, axis=2)
    numerator = jnp.einsum(
        "sht,stc->shc", weights.astype(BF), latent_cache[:, :, :LAT], preferred_element_type=F32
    )

    def mine(a):
        return lax.dynamic_slice_in_dim(a, core * heads, heads, 1)

    def other(a):
        return lax.dynamic_slice_in_dim(a, (1 - core) * heads, heads, 1)

    far_numerator = shifted(other(numerator).astype(BF), "ep", 1).astype(F32)
    far_stats = shifted(jnp.stack([other(peak), other(total)]), "ep", 1)
    near_peak, far_peak = mine(peak), far_stats[0]
    both = jnp.maximum(near_peak, far_peak)
    near_scale, far_scale = jnp.exp(near_peak - both), jnp.exp(far_peak - both)
    denominator = near_scale * mine(total) + far_scale * far_stats[1]
    combined = (
        near_scale[:, :, None] * mine(numerator) + far_scale[:, :, None] * far_numerator
    )
    return (combined / denominator[:, :, None]).astype(BF)


def local(
    queries,
    latent_cache,
    cache_lens,
    movers,
    hidden,
    norm_gain,
    routes,
    gate_weights,
    gate_proj,
    up_proj,
    down_proj,
):
    requests, model_width = hidden.shape
    half = model_width // 2
    core = lax.axis_index("ep")
    x_index = lax.axis_index("x")

    widened = hidden.astype(F32)
    inverse = lax.rsqrt(jnp.mean(widened * widened, axis=1, keepdims=True) + 1e-06)
    own_hidden = lax.dynamic_slice_in_dim(hidden, core * half, half, 1).astype(F32)
    own_gain = lax.dynamic_slice_in_dim(norm_gain, core * half, half, 0)
    normed = (own_hidden * inverse * own_gain).astype(BF)
    flat_routes = routes.reshape(-1)
    onehot = (flat_routes[:, None] == jnp.arange(EXPERTS, dtype=jnp.int32)[None, :]).astype(
        jnp.int32
    )
    earlier = jnp.cumsum(onehot, axis=0) - onehot
    slot_index = jnp.sum(earlier * onehot, axis=1)
    target = (flat_routes * CAP + slot_index).reshape(routes.shape)
    columns = jnp.arange(EXPERTS * CAP, dtype=jnp.int32)
    matches = target[:, :, None] == columns[None, None, :]
    placement = jnp.any(matches, axis=1).astype(BF)
    combine = jnp.sum(
        jnp.where(matches, gate_weights[:, :, None].astype(F32), 0.0), axis=1
    ).astype(BF)

    def swap_weights(w):
        far = lax.dynamic_slice_in_dim(w, (1 - core) * half, half, 0)
        return shifted(far, "ep", 1)

    near_gate = lax.dynamic_slice_in_dim(gate_proj[0], core * half, half, 0)
    near_up = lax.dynamic_slice_in_dim(up_proj[0], core * half, half, 0)
    mixed = jnp.concatenate(
        [near_gate, near_up, swap_weights(gate_proj[0]), swap_weights(up_proj[0])], axis=1
    )

    def down_rows(which):
        parts = []
        for by in range(4):
            source = (x_index - by) % 4
            parts.append(
                lax.dynamic_slice_in_dim(down_proj[0], source * 256 + which * 128, 128, 0)
            )
        return jnp.concatenate(parts, axis=0)

    near_down, far_down = down_rows(core), down_rows(1 - core)

    width = half // CHUNKS
    total = None
    attention = None
    for k in range(CHUNKS):
        part = normed[:, k * width : (k + 1) * width]
        outbound = jnp.einsum("rs,rd->sd", placement, part, preferred_element_type=F32)
        outbound = outbound.astype(BF).reshape(EXPERTS, CAP, width)
        arrived = lax.all_to_all(outbound, PLANE, split_axis=0, concat_axis=0, tiled=True)
        rows = lax.all_gather(arrived.reshape(EXPERTS * CAP, width), "x", axis=0, tiled=True)
        if k == CHUNKS - 1:
            attention = attend(queries, latent_cache, cache_lens, core)
            rows, attention = lax.optimization_barrier((rows, attention))
        product = jnp.dot(
            rows, mixed[k * width : (k + 1) * width], preferred_element_type=F32
        )
        total = product if total is None else total + product

    arrived = shifted(total[:, 256:], "ep", 1)
    value = total[:, :256] + arrived
    activated = (jax.nn.silu(value[:, :128]) * value[:, 128:]).astype(BF)
    blocks = [activated] + [shifted(activated, "x", by) for by in (1, 2, 3)]
    near = jnp.concatenate(blocks, axis=1)
    far = shifted(near, "ep", 1)
    expert_out = (
        jnp.dot(near, near_down, preferred_element_type=F32)
        + jnp.dot(far, far_down, preferred_element_type=F32)
    ).astype(BF)
    returned = lax.all_to_all(
        expert_out.reshape(4 * EXPERTS, CAP, -1),
        ("x",) + PLANE,
        split_axis=0,
        concat_axis=0,
        tiled=True,
    )
    weighted = jnp.einsum(
        "rk,qkd->rqd",
        combine,
        returned.reshape(4, EXPERTS * CAP, -1),
        preferred_element_type=F32,
    ).reshape(requests, half)
    expert_mix = (own_hidden + weighted).astype(BF)

    listed = movers[0]
    slot_ids = jnp.arange(requests, dtype=jnp.int32)
    flagged = jnp.any(slot_ids[:, None] == listed[None, :], axis=1)
    nothing = jnp.zeros((), BF)
    moved = jnp.where(
        (listed < requests)[:, None, None], attention[jnp.minimum(listed, requests - 1)], nothing
    )
    arrived_contexts = shifted(moved, "z", 4)
    served = jnp.concatenate(
        [jnp.where(flagged[:, None, None], nothing, attention), arrived_contexts], axis=0
    )
    return served, expert_mix


def solution(mesh):
    grid = Mesh(mesh.devices.reshape(8, 4, 4, 2), ("z", "y", "x", "ep"))
    dp = ("z", "y", "x")
    placed = (
        P(dp, None, None),
        P(dp, "ep", None),
        P(dp),
        P(dp, None),
        P(dp, None),
        P(),
        P(dp, None),
        P(dp, None),
        P(dp, None, "ep"),
        P(dp, None, "ep"),
        P(dp, None, "ep"),
    )
    return jax.shard_map(
        local,
        mesh=grid,
        in_specs=placed,
        out_specs=(P(dp, "ep", None), P(dp, "ep")),
        check_vma=False,
    )
```

```python
import jax
import jax.numpy as jnp
from jax import lax
from jax.experimental import pallas as pl
from jax.experimental.pallas import tpu as pltpu
from jax.sharding import Mesh, PartitionSpec as P

LAT = 512
EXPERTS = 32
CAP = 8
PLANE = ("z", "y")
SOFTMAX_SCALE = 192 ** (-0.5)
BATCHES = ((0, 1, -1), (2, 3, -2, -3, 4))
BF = jnp.bfloat16
F32 = jnp.float32


def shifted(x, axis, by):
    devices = lax.axis_size(axis)
    return lax.ppermute(x, axis, [(i, (i + by) % devices) for i in range(devices)])


def attend(queries, latent_cache, lengths, core):
    span = latent_cache.shape[1]
    heads = queries.shape[1] // 2
    scores = jnp.einsum("shc,stc->sht", queries, latent_cache, preferred_element_type=F32)
    scores = scores * SOFTMAX_SCALE
    positions = core * span + jnp.arange(span, dtype=jnp.int32)
    valid = positions[None, None, :] < lengths[:, None, None]
    masked = jnp.where(valid, scores, -1e30)
    peak = jnp.max(masked, axis=2)
    weights = jnp.where(valid, jnp.exp(masked - peak[:, :, None]), 0.0)
    total = jnp.sum(weights, axis=2)
    numerator = jnp.einsum(
        "sht,stc->shc", weights.astype(BF), latent_cache[:, :, :LAT], preferred_element_type=F32
    )

    def mine(a):
        return lax.dynamic_slice_in_dim(a, core * heads, heads, 1)

    def other(a):
        return lax.dynamic_slice_in_dim(a, (1 - core) * heads, heads, 1)

    far_numerator = shifted(other(numerator).astype(BF), "ep", 1).astype(F32)
    far_stats = shifted(jnp.stack([other(peak), other(total)]), "ep", 1)
    near_peak, far_peak = mine(peak), far_stats[0]
    both = jnp.maximum(near_peak, far_peak)
    near_scale, far_scale = jnp.exp(near_peak - both), jnp.exp(far_peak - both)
    denominator = near_scale * mine(total) + far_scale * far_stats[1]
    combined = (
        near_scale[:, :, None] * mine(numerator) + far_scale[:, :, None] * far_numerator
    )
    return (combined / denominator[:, :, None]).astype(BF)


def pack_rows(core, hidden, norm_gain, routes):
    requests, model_width = hidden.shape
    half = model_width // 2

    def kernel(core_ref, all_ref, half_ref, gain_ref, routes_ref, packed_ref):
        del core_ref
        wide = all_ref[...].astype(F32)
        inverse = lax.rsqrt(jnp.mean(wide * wide, axis=1, keepdims=True) + 1e-06)
        normed = half_ref[...].astype(F32) * inverse * gain_ref[...]
        packed_ref[:, :half] = normed.astype(BF)
        named = routes_ref[...].astype(F32)
        fill = jnp.full((requests, 128 - named.shape[1]), -1.0, F32)
        packed_ref[:, half:] = jnp.concatenate([named, fill], axis=1).astype(BF)

    return pl.pallas_call(
        kernel,
        out_shape=jax.ShapeDtypeStruct((requests, half + 128), BF),
        grid_spec=pltpu.PrefetchScalarGridSpec(
            num_scalar_prefetch=1,
            grid=(1,),
            in_specs=[
                pl.BlockSpec((requests, model_width), lambda i, c: (0, 0)),
                pl.BlockSpec((requests, half), lambda i, c: (0, c[0])),
                pl.BlockSpec((1, half), lambda i, c: (0, c[0])),
                pl.BlockSpec(routes.shape, lambda i, c: (0, 0)),
            ],
            out_specs=pl.BlockSpec((requests, half + 128), lambda i, c: (0, 0)),
        ),
    )(core.reshape(1), hidden, hidden, norm_gain.reshape(1, -1), routes)


def choose_rows(places, blocks):
    count = len(blocks)
    half = blocks[0].shape[1] - 128
    rows = sum(block.shape[0] for block in blocks)
    span = rows // 16 * CAP
    lanes = 4 * span

    def kernel(places_ref, *refs):
        sources, outs = refs[:count], refs[count:]
        base, y_index = places_ref[0], places_ref[1]
        ids = jnp.concatenate([ref[:, half:] for ref in sources], axis=0).astype(F32)
        lane = lax.broadcasted_iota(jnp.int32, (rows, lanes), 1)
        row_block = lax.broadcasted_iota(jnp.int32, (rows, lanes), 0) >> 4
        step = sum((lane >= n * span).astype(jnp.int32) for n in (1, 2, 3))
        within = lane - step * span
        expert = (base + ((y_index + step) & 3)).astype(F32)
        member = jnp.zeros((rows, lanes), F32)
        for k in range(8):
            member = member + jnp.where(ids[:, k : k + 1] == expert, 1.0, 0.0)
        left = lax.broadcasted_iota(jnp.int32, (rows, rows), 0)
        right = lax.broadcasted_iota(jnp.int32, (rows, rows), 1)
        lower = jnp.where((right < left) & (right >> 4 == left >> 4), 1.0, 0.0)
        slot = jnp.dot(lower.astype(BF), member.astype(BF), preferred_element_type=F32)
        spot = (within & 7).astype(F32)
        fits = (member > 0.5) & (slot == spot) & (row_block == within >> 3)
        chosen = jnp.where(fits, 1.0, 0.0).astype(BF)
        for start in range(0, half, 512):
            columns = slice(start, start + 512)
            data = jnp.concatenate([ref[:, columns] for ref in sources], axis=0)
            picked = lax.dot_general(
                chosen, data, (((0,), (0,)), ((), ())), preferred_element_type=F32
            )
            for n in range(4):
                outs[n][:, columns] = picked[n * span : (n + 1) * span].astype(BF)

    shape = jax.ShapeDtypeStruct((span, half), BF)
    vmem = pl.BlockSpec(memory_space=pltpu.VMEM)
    return pl.pallas_call(
        kernel,
        out_shape=(shape,) * 4,
        in_specs=[pl.BlockSpec(memory_space=pltpu.SMEM)] + [vmem] * count,
        out_specs=(vmem,) * 4,
    )(places, *blocks)


def local(
    queries,
    latent_cache,
    cache_lens,
    movers,
    hidden,
    norm_gain,
    routes,
    gate_weights,
    gate_proj,
    up_proj,
    down_proj,
):
    requests, model_width = hidden.shape
    half = model_width // 2
    core = lax.axis_index("ep")
    x_index, y_index, z_index = (lax.axis_index(name) for name in ("x", "y", "z"))
    packed = pack_rows(core, hidden, norm_gain, routes)

    places = jnp.stack([z_index * 4, y_index]).astype(jnp.int32)
    after, before = shifted(packed, "z", 1), shifted(packed, "z", -1)
    opposite = shifted(packed, "z", 4)
    upward = shifted(jnp.concatenate([packed, after], axis=0), "z", 2)
    downward = shifted(jnp.concatenate([packed, before], axis=0), "z", -2)

    def weights_for_half(gate, up):
        both = jnp.concatenate([gate, up], axis=1)
        far = lax.dynamic_slice_in_dim(both, (1 - core) * half, half, 0)
        near = lax.dynamic_slice_in_dim(both, core * half, half, 0)
        return jnp.concatenate([near, shifted(far, "ep", 1)], axis=1)

    def along_y(picked):
        parts = [picked[0]] + [shifted(picked[by], "y", by) for by in (1, 2, 3)]
        return jnp.concatenate(parts, axis=0)

    first = choose_rows(places, [packed, after, before])
    first, opposite, gate_proj, up_proj = lax.optimization_barrier(
        (first, opposite, gate_proj, up_proj)
    )
    batches = [along_y(first)]
    mixed = weights_for_half(gate_proj[0], up_proj[0])
    batches[0], upward, downward, mixed = lax.optimization_barrier(
        (batches[0], upward, downward, mixed)
    )
    second = choose_rows(places, [upward, downward, opposite])
    batches.append(along_y(second))

    ahead = [shifted(b, "x", 1) for b in batches]
    behind = [shifted(b, "x", -1) for b in batches]
    across = []
    for a, b in zip(ahead, behind):
        middle = a.shape[0] // 2
        across += [shifted(a[:middle], "x", 1), shifted(b[middle:], "x", -1)]

    routes, gate_weights, down_proj, hidden, queries, latent_cache, movers, _ = (
        lax.optimization_barrier(
            (routes, gate_weights, down_proj, hidden, queries, latent_cache, movers, second[0])
        )
    )
    own_hidden = lax.dynamic_slice_in_dim(hidden, core * half, half, 1).astype(F32)
    strictly_lower = jnp.tril(jnp.ones((requests, requests), F32), -1)

    attention = attend(queries, latent_cache, cache_lens, core)
    listed = movers[0]
    slot_ids = jnp.arange(requests, dtype=jnp.int32)
    flagged = jnp.any(slot_ids[:, None] == listed[None, :], axis=1)
    nothing = jnp.zeros((), BF)
    picks = (listed[:, None] == slot_ids[None, :]).astype(BF)
    moved = jnp.einsum("mr,rhd->mhd", picks, attention, preferred_element_type=F32).astype(BF)
    arrived_contexts = shifted(moved, "z", 4)
    served = jnp.concatenate(
        [jnp.where(flagged[:, None, None], nothing, attention), arrived_contexts], axis=0
    )

    spread = jnp.arange(EXPERTS, dtype=jnp.int32)
    hits = routes[:, :, None] == spread[None, None, :]
    member = jnp.any(hits, axis=1).astype(F32)
    gates = jnp.sum(jnp.where(hits, gate_weights[:, :, None].astype(F32), 0.0), axis=1)
    slot = jnp.dot(strictly_lower, member)
    at_slot = slot[:, :, None] == jnp.arange(CAP, dtype=F32)[None, None, :]
    combine = jnp.where(at_slot, gates[:, :, None], 0.0)
    combine = combine.astype(BF).reshape(requests, EXPERTS * CAP)

    def down_rows(which):
        parts = []
        for by in range(4):
            source = (x_index + by) % 4
            parts.append(
                lax.dynamic_slice_in_dim(down_proj[0], source * 256 + which * 128, 128, 0)
            )
        return jnp.concatenate(parts, axis=0)

    near_down, far_down = down_rows(core), down_rows(1 - core)

    near_by = jnp.array([by for ds in BATCHES for _ in range(4) for by in ds], jnp.int32)
    near_y = jnp.array([n for ds in BATCHES for n in range(4) for _ in ds], jnp.int32)
    homes = (z_index - near_by) % 8 * 4 + (y_index - near_y) % 4
    homes = (homes[:, None] * CAP + jnp.arange(CAP, dtype=jnp.int32)[None, :]).reshape(-1)
    order = (jnp.arange(EXPERTS * CAP, dtype=jnp.int32)[:, None] == homes[None, :]).astype(BF)

    def activate(blocks):
        total = [jnp.dot(b, mixed, preferred_element_type=F32) for b in blocks]
        total = jnp.concatenate(total, axis=0)
        value = total[:, :256] + shifted(total[:, 256:], "ep", 1)
        activated = (jax.nn.silu(value[:, :128]) * value[:, 128:]).astype(BF)
        count = activated.shape[0] // (EXPERTS * CAP)
        activated = activated.reshape(count, EXPERTS * CAP, 128)
        return jnp.einsum("ij,njd->nid", order, activated, preferred_element_type=F32).astype(BF)

    def spread_along_x(activated):
        return [activated] + [shifted(activated, "x", -by) for by in (1, 2, 3)]

    own = spread_along_x(activate(batches))
    near = spread_along_x(activate([ahead[0], ahead[1], behind[0], behind[1]]))
    far_rows = jnp.concatenate(across, axis=0)
    far = spread_along_x(activate([far_rows]))
    by_home = [
        [a[0] for a in own],
        [a[1] for a in near],
        [a[0] for a in far],
        [a[0] for a in near],
    ]
    stripes = [
        jnp.concatenate([by_home[(r - s) % 4][s] for s in range(4)], axis=1) for r in range(4)
    ]
    twice = jnp.concatenate(stripes + stripes[:3], axis=0)
    count = EXPERTS * CAP
    joined = lax.dynamic_slice_in_dim(twice, (4 - x_index) % 4 * count, 4 * count, 0)
    expert_out = (
        jnp.dot(joined, near_down, preferred_element_type=F32)
        + jnp.dot(shifted(joined, "ep", 1), far_down, preferred_element_type=F32)
    ).astype(BF)
    expert_out, served, own_hidden = lax.optimization_barrier((expert_out, served, own_hidden))
    returned = lax.all_to_all(
        expert_out.reshape(4 * EXPERTS, CAP, -1),
        ("x",) + PLANE,
        split_axis=0,
        concat_axis=0,
        tiled=True,
    )
    returned = lax.optimization_barrier(returned)
    weighted = jnp.einsum(
        "rk,qkd->rqd",
        combine,
        returned.reshape(4, count, -1),
        preferred_element_type=F32,
    ).reshape(requests, half)
    expert_mix = (own_hidden + weighted).astype(BF)
    return served, expert_mix


def solution(mesh):
    grid = Mesh(mesh.devices.reshape(8, 4, 4, 2), ("z", "y", "x", "ep"))
    dp = ("z", "y", "x")
    placed = (
        P(dp, None, None),
        P(dp, "ep", None),
        P(dp),
        P(dp, None),
        P(dp, None),
        P(),
        P(dp, None),
        P(dp, None),
        P(dp, None, "ep"),
        P(dp, None, "ep"),
        P(dp, None, "ep"),
    )
    return jax.shard_map(
        local,
        mesh=grid,
        in_specs=placed,
        out_specs=(P(dp, "ep", None), P(dp, "ep")),
        check_vma=False,
    )
```

```python
import jax
import jax.numpy as jnp
from jax import lax
from jax.experimental import pallas as pl
from jax.experimental.pallas import tpu as pltpu
from jax.sharding import Mesh, PartitionSpec as P

LAT = 512
EXPERTS = 32
CAP = 8
PLANE = ("z", "y")
SOFTMAX_SCALE = 192 ** (-0.5)
BF = jnp.bfloat16
F32 = jnp.float32


def shifted(x, axis, by):
    devices = lax.axis_size(axis)
    return lax.ppermute(x, axis, [(i, (i + by) % devices) for i in range(devices)])


def attend(queries, latent_cache, lengths, core):
    span = latent_cache.shape[1]
    heads = queries.shape[1] // 2
    scores = jnp.einsum("shc,stc->sht", queries, latent_cache, preferred_element_type=F32)
    scores = scores * SOFTMAX_SCALE
    positions = core * span + jnp.arange(span, dtype=jnp.int32)
    valid = positions[None, None, :] < lengths[:, None, None]
    masked = jnp.where(valid, scores, -1e30)
    peak = jnp.max(masked, axis=2)
    weights = jnp.where(valid, jnp.exp(masked - peak[:, :, None]), 0.0)
    total = jnp.sum(weights, axis=2)
    numerator = jnp.einsum(
        "sht,stc->shc", weights.astype(BF), latent_cache[:, :, :LAT], preferred_element_type=F32
    )

    def mine(a):
        return lax.dynamic_slice_in_dim(a, core * heads, heads, 1)

    def other(a):
        return lax.dynamic_slice_in_dim(a, (1 - core) * heads, heads, 1)

    far_numerator = shifted(other(numerator).astype(BF), "ep", 1).astype(F32)
    far_stats = shifted(jnp.stack([other(peak), other(total)]), "ep", 1)
    near_peak, far_peak = mine(peak), far_stats[0]
    both = jnp.maximum(near_peak, far_peak)
    near_scale, far_scale = jnp.exp(near_peak - both), jnp.exp(far_peak - both)
    denominator = near_scale * mine(total) + far_scale * far_stats[1]
    combined = (
        near_scale[:, :, None] * mine(numerator) + far_scale[:, :, None] * far_numerator
    )
    return (combined / denominator[:, :, None]).astype(BF)


def slot_rows(core, hidden, norm_gain, routes, gate_weights):
    requests, model_width = hidden.shape
    half = model_width // 2
    slots = EXPERTS * CAP

    def kernel(core_ref, all_ref, half_ref, gain_ref, routes_ref, gates_ref, out_ref, mix_ref):
        del core_ref
        ids = routes_ref[...].astype(F32)
        gates = gates_ref[...].astype(F32)
        lane = lax.broadcasted_iota(jnp.int32, (requests, slots), 1)
        expert = (lane >> 3).astype(F32)
        member = jnp.zeros((requests, slots), F32)
        weight = jnp.zeros((requests, slots), F32)
        for k in range(routes.shape[1]):
            hit = ids[:, k : k + 1] == expert
            member = jnp.where(hit, 1.0, member)
            weight = jnp.where(hit, gates[:, k : k + 1], weight)
        left = lax.broadcasted_iota(jnp.int32, (requests, requests), 0)
        right = lax.broadcasted_iota(jnp.int32, (requests, requests), 1)
        lower = jnp.where(right < left, 1.0, 0.0).astype(BF)
        earlier = jnp.dot(lower, member.astype(BF), preferred_element_type=F32)
        fits = (member > 0.5) & (earlier == (lane & 7).astype(F32))
        mix_ref[...] = jnp.where(fits, weight, 0.0).astype(BF)
        chosen = jnp.where(fits, 1.0, 0.0).astype(BF)
        wide = all_ref[...].astype(F32)
        inverse = lax.rsqrt(jnp.mean(wide * wide, axis=1, keepdims=True) + 1e-06)
        for start in range(0, half, 512):
            columns = slice(start, start + 512)
            normed = half_ref[:, columns].astype(F32) * inverse * gain_ref[:, columns]
            out_ref[:, columns] = lax.dot_general(
                chosen, normed.astype(BF), (((0,), (0,)), ((), ())), preferred_element_type=F32
            ).astype(BF)

    return pl.pallas_call(
        kernel,
        out_shape=(
            jax.ShapeDtypeStruct((slots, half), BF),
            jax.ShapeDtypeStruct((requests, slots), BF),
        ),
        grid_spec=pltpu.PrefetchScalarGridSpec(
            num_scalar_prefetch=1,
            grid=(1,),
            in_specs=[
                pl.BlockSpec((requests, model_width), lambda i, c: (0, 0)),
                pl.BlockSpec((requests, half), lambda i, c: (0, c[0])),
                pl.BlockSpec((1, half), lambda i, c: (0, c[0])),
                pl.BlockSpec(routes.shape, lambda i, c: (0, 0)),
                pl.BlockSpec(gate_weights.shape, lambda i, c: (0, 0)),
            ],
            out_specs=(
                pl.BlockSpec((slots, half), lambda i, c: (0, 0)),
                pl.BlockSpec((requests, slots), lambda i, c: (0, 0)),
            ),
        ),
    )(core.reshape(1), hidden, hidden, norm_gain.reshape(1, -1), routes, gate_weights)


def local(
    queries,
    latent_cache,
    cache_lens,
    movers,
    hidden,
    norm_gain,
    routes,
    gate_weights,
    gate_proj,
    up_proj,
    down_proj,
):
    requests, model_width = hidden.shape
    half = model_width // 2
    count = EXPERTS * CAP
    core = lax.axis_index("ep")
    x_index = lax.axis_index("x")

    outbound, combine = slot_rows(core, hidden, norm_gain, routes, gate_weights)
    rows = lax.all_to_all(
        outbound.reshape(EXPERTS, CAP, half), PLANE, split_axis=0, concat_axis=0, tiled=True
    ).reshape(count, half)

    ahead, behind = shifted(rows, "x", 1), shifted(rows, "x", -1)
    rows, gate_proj, up_proj, down_proj, hidden, queries, latent_cache, movers = (
        lax.optimization_barrier(
            (rows, gate_proj, up_proj, down_proj, hidden, queries, latent_cache, movers)
        )
    )

    both = jnp.concatenate([gate_proj[0], up_proj[0]], axis=1)
    far_weights = lax.dynamic_slice_in_dim(both, (1 - core) * half, half, 0)
    near_weights = lax.dynamic_slice_in_dim(both, core * half, half, 0)
    mixed = jnp.concatenate([near_weights, shifted(far_weights, "ep", 1)], axis=1)

    attention = attend(queries, latent_cache, cache_lens, core)
    listed = movers[0]
    slot_ids = jnp.arange(requests, dtype=jnp.int32)
    flagged = jnp.any(slot_ids[:, None] == listed[None, :], axis=1)
    nothing = jnp.zeros((), BF)
    picks = (listed[:, None] == slot_ids[None, :]).astype(BF)
    moved = jnp.einsum("mr,rhd->mhd", picks, attention, preferred_element_type=F32).astype(BF)
    arrived_contexts = shifted(moved, "z", 4)
    served = jnp.concatenate(
        [jnp.where(flagged[:, None, None], nothing, attention), arrived_contexts], axis=0
    )

    def down_rows(which):
        parts = []
        for by in range(4):
            source = (x_index + by) % 4
            parts.append(
                lax.dynamic_slice_in_dim(down_proj[0], source * 256 + which * 128, 128, 0)
            )
        return jnp.concatenate(parts, axis=0)

    near_down, far_down = down_rows(core), down_rows(1 - core)

    def activate(blocks):
        total = [jnp.dot(b, mixed, preferred_element_type=F32) for b in blocks]
        total = jnp.concatenate(total, axis=0)
        value = total[:, :256] + shifted(total[:, 256:], "ep", 1)
        activated = (jax.nn.silu(value[:, :128]) * value[:, 128:]).astype(BF)
        return activated.reshape(-1, count, 128)

    def spread_along_x(activated):
        return [activated] + [shifted(activated, "x", -by) for by in (1, 2, 3)]

    own = spread_along_x(activate([rows]))
    ahead, behind, own, served = lax.optimization_barrier((ahead, behind, own, served))
    middle = count // 2
    across = [shifted(ahead[:middle], "x", 1), shifted(behind[middle:], "x", -1)]
    near = spread_along_x(activate([ahead, behind]))
    across, near = lax.optimization_barrier((across, near))
    far = spread_along_x(activate([jnp.concatenate(across, axis=0)]))

    by_home = [
        [a[0] for a in own],
        [a[1] for a in near],
        [a[0] for a in far],
        [a[0] for a in near],
    ]
    stripes = [
        jnp.concatenate([by_home[(r - s) % 4][s] for s in range(4)], axis=1) for r in range(4)
    ]
    twice = jnp.concatenate(stripes + stripes[:3], axis=0)
    joined = lax.dynamic_slice_in_dim(twice, (4 - x_index) % 4 * count, 4 * count, 0)
    expert_out = (
        jnp.dot(joined, near_down, preferred_element_type=F32)
        + jnp.dot(shifted(joined, "ep", 1), far_down, preferred_element_type=F32)
    ).astype(BF)
    returned = lax.all_to_all(
        expert_out.reshape(4 * EXPERTS, CAP, -1),
        ("x",) + PLANE,
        split_axis=0,
        concat_axis=0,
        tiled=True,
    )
    weighted = jnp.einsum(
        "rk,qkd->rqd",
        combine,
        returned.reshape(4, count, -1),
        preferred_element_type=F32,
    ).reshape(requests, half)
    own_hidden = lax.dynamic_slice_in_dim(hidden, core * half, half, 1).astype(F32)
    expert_mix = (own_hidden + weighted).astype(BF)
    return served, expert_mix


def solution(mesh):
    grid = Mesh(mesh.devices.reshape(8, 4, 4, 2), ("z", "y", "x", "ep"))
    dp = ("z", "y", "x")
    placed = (
        P(dp, None, None),
        P(dp, "ep", None),
        P(dp),
        P(dp, None),
        P(dp, None),
        P(),
        P(dp, None),
        P(dp, None),
        P(dp, None, "ep"),
        P(dp, None, "ep"),
        P(dp, None, "ep"),
    )
    return jax.shard_map(
        local,
        mesh=grid,
        in_specs=placed,
        out_specs=(P(dp, "ep", None), P(dp, "ep")),
        check_vma=False,
    )
```

```python
import jax
import jax.numpy as jnp
from jax import lax
from jax.experimental import pallas as pl
from jax.experimental.pallas import tpu as pltpu
from jax.sharding import Mesh, PartitionSpec as P

LAT = 512
EXPERTS = 32
CAP = 8
AWAY = (0, 1, 7, 4, 2, 3, 6, 5)
SOFTMAX_SCALE = 192 ** (-0.5)
BF = jnp.bfloat16
F32 = jnp.float32


def shifted(x, axis, by):
    devices = lax.axis_size(axis)
    return lax.ppermute(x, axis, [(i, (i + by) % devices) for i in range(devices)])


def attend(queries, latent_cache, lengths, core):
    span = latent_cache.shape[1]
    heads = queries.shape[1] // 2
    scores = jnp.einsum("shc,stc->sht", queries, latent_cache, preferred_element_type=F32)
    scores = scores * SOFTMAX_SCALE
    positions = core * span + jnp.arange(span, dtype=jnp.int32)
    valid = positions[None, None, :] < lengths[:, None, None]
    masked = jnp.where(valid, scores, -1e30)
    peak = jnp.max(masked, axis=2)
    weights = jnp.where(valid, jnp.exp(masked - peak[:, :, None]), 0.0)
    total = jnp.sum(weights, axis=2)
    numerator = jnp.einsum(
        "sht,stc->shc", weights.astype(BF), latent_cache[:, :, :LAT], preferred_element_type=F32
    )

    def mine(a):
        return lax.dynamic_slice_in_dim(a, core * heads, heads, 1)

    def other(a):
        return lax.dynamic_slice_in_dim(a, (1 - core) * heads, heads, 1)

    far_numerator = shifted(other(numerator).astype(BF), "ep", 1).astype(F32)
    far_stats = shifted(jnp.stack([other(peak), other(total)]), "ep", 1)
    near_peak, far_peak = mine(peak), far_stats[0]
    both = jnp.maximum(near_peak, far_peak)
    near_scale, far_scale = jnp.exp(near_peak - both), jnp.exp(far_peak - both)
    denominator = near_scale * mine(total) + far_scale * far_stats[1]
    combined = (
        near_scale[:, :, None] * mine(numerator) + far_scale[:, :, None] * far_numerator
    )
    return (combined / denominator[:, :, None]).astype(BF)


def pack_rows(core, hidden, norm_gain, routes, gate_weights):
    requests, model_width = hidden.shape
    half = model_width // 2
    slots = EXPERTS * CAP
    top = routes.shape[1]

    def kernel(
        core_ref, all_ref, half_ref, gain_ref, routes_ref, ids_ref, gates_ref, out_ref, mix_ref
    ):
        del core_ref
        wide = all_ref[...].astype(F32)
        inverse = lax.rsqrt(jnp.mean(wide * wide, axis=1, keepdims=True) + 1e-06)
        normed = half_ref[...].astype(F32) * inverse * gain_ref[...]
        out_ref[:, :half] = normed.astype(BF)
        named = routes_ref[...].astype(F32)
        fill = jnp.full((requests, 128 - top), -1.0, F32)
        out_ref[:, half:] = jnp.concatenate([named, fill], axis=1).astype(BF)
        ids = ids_ref[...].astype(F32)
        gates = gates_ref[...].astype(F32)
        place = lax.broadcasted_iota(jnp.int32, (slots, requests), 0)
        expert = (((place >> 3) & 7) * 4 + (place >> 6)).astype(F32)
        member = jnp.zeros((slots, requests), F32)
        weight = jnp.zeros((slots, requests), F32)
        for k in range(top):
            hit = ids[k : k + 1, :] == expert
            member = jnp.where(hit, 1.0, member)
            weight = jnp.where(hit, gates[k : k + 1, :], weight)
        left = lax.broadcasted_iota(jnp.int32, (requests, requests), 0)
        right = lax.broadcasted_iota(jnp.int32, (requests, requests), 1)
        before = jnp.where(left < right, 1.0, 0.0).astype(BF)
        earlier = jnp.dot(member.astype(BF), before, preferred_element_type=F32)
        fits = (member > 0.5) & (earlier == (place & 7).astype(F32))
        mix_ref[...] = jnp.where(fits, weight, 0.0).astype(BF)

    return pl.pallas_call(
        kernel,
        out_shape=(
            jax.ShapeDtypeStruct((requests, half + 128), BF),
            jax.ShapeDtypeStruct((slots, requests), BF),
        ),
        grid_spec=pltpu.PrefetchScalarGridSpec(
            num_scalar_prefetch=1,
            grid=(1,),
            in_specs=[
                pl.BlockSpec((requests, model_width), lambda i, c: (0, 0)),
                pl.BlockSpec((requests, half), lambda i, c: (0, c[0])),
                pl.BlockSpec((1, half), lambda i, c: (0, c[0])),
                pl.BlockSpec((requests, top), lambda i, c: (0, 0)),
                pl.BlockSpec((top, requests), lambda i, c: (0, 0)),
                pl.BlockSpec((top, requests), lambda i, c: (0, 0)),
            ],
            out_specs=(
                pl.BlockSpec((requests, half + 128), lambda i, c: (0, 0)),
                pl.BlockSpec((slots, requests), lambda i, c: (0, 0)),
            ),
        ),
    )(
        core.reshape(1),
        hidden,
        hidden,
        norm_gain.reshape(1, -1),
        routes,
        routes.T,
        gate_weights.T,
    )


def choose_rows(z_index, blocks):
    count = len(blocks)
    half = blocks[0].shape[1] - 128
    rows = 8 * 16
    span = 4 * CAP
    lanes = 8 * span

    def kernel(z_ref, *refs):
        sources, outs = refs[:count], refs[count:]
        z = z_ref[0]
        ids = jnp.concatenate([ref[:, half:] for ref in sources], axis=0).astype(F32)
        lane = lax.broadcasted_iota(jnp.int32, (rows, lanes), 1)
        block = lax.broadcasted_iota(jnp.int32, (rows, lanes), 0) >> 4
        away = sum(jnp.where(block == n, by, 0) for n, by in enumerate(AWAY))
        rank = (lane >> 7) * 4 + ((lane >> 3) & 3)
        expert = (z * 4 + ((lane >> 5) & 3)).astype(F32)
        member = jnp.zeros((rows, lanes), F32)
        for k in range(8):
            member = jnp.where(ids[:, k : k + 1] == expert, 1.0, member)
        left = lax.broadcasted_iota(jnp.int32, (rows, rows), 0)
        right = lax.broadcasted_iota(jnp.int32, (rows, rows), 1)
        lower = jnp.where((right < left) & (right >> 4 == left >> 4), 1.0, 0.0)
        slot = jnp.dot(lower.astype(BF), member.astype(BF), preferred_element_type=F32)
        fits = (member > 0.5) & (slot == (lane & 7).astype(F32))
        fits = fits & (rank == ((z + 8 - away) & 7))
        chosen = jnp.where(fits, 1.0, 0.0).astype(BF)
        for start in range(0, half, 512):
            columns = slice(start, start + 512)
            data = jnp.concatenate([ref[:, columns] for ref in sources], axis=0)
            picked = lax.dot_general(
                chosen, data, (((0,), (0,)), ((), ())), preferred_element_type=F32
            ).astype(BF)
            for n in range(8):
                outs[n // 4][n % 4, :, columns] = picked[n * span : (n + 1) * span]

    shape = jax.ShapeDtypeStruct((4, span, half), BF)
    vmem = pl.BlockSpec(memory_space=pltpu.VMEM)
    return pl.pallas_call(
        kernel,
        out_shape=(shape,) * 2,
        in_specs=[pl.BlockSpec(memory_space=pltpu.SMEM)] + [vmem] * count,
        out_specs=(vmem,) * 2,
    )(z_index.reshape(1), *blocks)


def add_experts(core, hidden, mix, returned):
    requests = hidden.shape[0]
    blocks, slots, width = returned.shape

    def kernel(core_ref, hidden_ref, mix_ref, returned_ref, out_ref):
        del core_ref
        weighted = lax.dot_general(
            mix_ref[...],
            returned_ref[0],
            (((0,), (0,)), ((), ())),
            preferred_element_type=F32,
        )
        out_ref[...] = (hidden_ref[...].astype(F32) + weighted).astype(BF)

    return pl.pallas_call(
        kernel,
        out_shape=jax.ShapeDtypeStruct((requests, blocks * width), BF),
        grid_spec=pltpu.PrefetchScalarGridSpec(
            num_scalar_prefetch=1,
            grid=(blocks,),
            in_specs=[
                pl.BlockSpec((requests, width), lambda i, c: (0, c[0] * blocks + i)),
                pl.BlockSpec((slots, requests), lambda i, c: (0, 0)),
                pl.BlockSpec((1, slots, width), lambda i, c: (i, 0, 0)),
            ],
            out_specs=pl.BlockSpec((requests, width), lambda i, c: (0, i)),
        ),
    )(core.reshape(1), hidden, mix, returned)


def local(
    queries,
    latent_cache,
    cache_lens,
    movers,
    hidden,
    norm_gain,
    routes,
    gate_weights,
    gate_proj,
    up_proj,
    down_proj,
):
    requests, model_width = hidden.shape
    half = model_width // 2
    count = EXPERTS * CAP
    core = lax.axis_index("ep").astype(jnp.int32)
    x_index = lax.axis_index("x").astype(jnp.int32)

    z_index = lax.axis_index("z").astype(jnp.int32)
    packed, mix = pack_rows(core, hidden, norm_gain, routes, gate_weights)
    packed, gate_proj, up_proj, down_proj = lax.optimization_barrier(
        (packed, gate_proj, up_proj, down_proj)
    )
    after, before = shifted(packed, "z", 1), shifted(packed, "z", -1)
    opposite = shifted(packed, "z", 4)
    upward = shifted(jnp.concatenate([packed, after], axis=0), "z", 2)
    downward = shifted(jnp.concatenate([packed, before], axis=0), "z", -2)
    picked = choose_rows(z_index, [packed, after, before, opposite, upward, downward])
    low, high = [
        lax.all_to_all(part, "y", split_axis=0, concat_axis=0, tiled=True).reshape(-1, half)
        for part in picked
    ]

    both = jnp.concatenate([gate_proj[0], up_proj[0]], axis=1)
    far_weights = lax.dynamic_slice_in_dim(both, (1 - core) * half, half, 0)
    near_weights = lax.dynamic_slice_in_dim(both, core * half, half, 0)
    mixed = jnp.concatenate([near_weights, shifted(far_weights, "ep", 1)], axis=1)

    def down_rows(which):
        parts = []
        for by in range(4):
            source = (x_index + by) % 4
            parts.append(
                lax.dynamic_slice_in_dim(down_proj[0], source * 256 + which * 128, 128, 0)
            )
        return jnp.concatenate(parts, axis=0)

    near_down, far_down = down_rows(core), down_rows(1 - core)
    low, high, mixed, near_down, far_down, queries, latent_cache, movers = (
        lax.optimization_barrier(
            (low, high, mixed, near_down, far_down, queries, latent_cache, movers)
        )
    )

    ahead_low, behind_low = shifted(low, "x", 1), shifted(low, "x", -1)
    ahead_high, behind_high = shifted(high, "x", 1), shifted(high, "x", -1)
    across_low, across_high = shifted(ahead_low, "x", 1), shifted(behind_high, "x", -1)

    attention = attend(queries, latent_cache, cache_lens, core)
    listed = movers[0]
    slot_ids = jnp.arange(requests, dtype=jnp.int32)
    flagged = jnp.any(slot_ids[:, None] == listed[None, :], axis=1)
    nothing = jnp.zeros((), BF)
    picks = (listed[:, None] == slot_ids[None, :]).astype(BF)
    moved = jnp.einsum("mr,rhd->mhd", picks, attention, preferred_element_type=F32).astype(BF)
    arrived_contexts = shifted(moved, "z", 4)
    served = jnp.concatenate(
        [jnp.where(flagged[:, None, None], nothing, attention), arrived_contexts], axis=0
    )

    def products(blocks):
        return [jnp.dot(b, mixed, preferred_element_type=F32) for b in blocks]

    def activate(totals):
        total = jnp.concatenate(totals, axis=0)
        value = total[:, :256] + shifted(total[:, 256:], "ep", 1)
        activated = (jax.nn.silu(value[:, :128]) * value[:, 128:]).astype(BF)
        activated = jnp.swapaxes(activated.reshape(-1, 2, 4, 4 * CAP, 128), 1, 2)
        return activated.reshape(-1, count, 128)

    own = activate(products([low, high]))
    ahead_low, ahead_high, behind_low, behind_high, own, served = lax.optimization_barrier(
        (ahead_low, ahead_high, behind_low, behind_high, own, served)
    )
    after_x = products([behind_low, behind_high])
    before_x = products([ahead_low, ahead_high])
    across_low, across_high, after_x, before_x = lax.optimization_barrier(
        (across_low, across_high, after_x, before_x)
    )
    others = activate(after_x + products([across_low, across_high]) + before_x)
    acts = jnp.concatenate([own, others], axis=0)
    held = [acts] + [shifted(acts, "x", -by) for by in (1, 2, 3)]
    stripes = [jnp.concatenate([held[s][(r - s) % 4] for s in range(4)], axis=1) for r in range(4)]
    twice = jnp.concatenate(stripes + stripes[:3], axis=0)
    joined = lax.dynamic_slice_in_dim(twice, (4 - x_index) % 4 * count, 4 * count, 0)
    expert_out = (
        jnp.dot(joined, near_down, preferred_element_type=F32)
        + jnp.dot(shifted(joined, "ep", 1), far_down, preferred_element_type=F32)
    ).astype(BF)
    returned = lax.all_to_all(
        expert_out.reshape(4 * EXPERTS, CAP, -1),
        ("x", "y", "z"),
        split_axis=0,
        concat_axis=0,
        tiled=True,
    )
    expert_mix = add_experts(core, hidden, mix, returned.reshape(4, count, -1))
    return served, expert_mix


def solution(mesh):
    grid = Mesh(mesh.devices.reshape(8, 4, 4, 2), ("z", "y", "x", "ep"))
    dp = ("z", "y", "x")
    placed = (
        P(dp, None, None),
        P(dp, "ep", None),
        P(dp),
        P(dp, None),
        P(dp, None),
        P(),
        P(dp, None),
        P(dp, None),
        P(dp, None, "ep"),
        P(dp, None, "ep"),
        P(dp, None, "ep"),
    )
    return jax.shard_map(
        local,
        mesh=grid,
        in_specs=placed,
        out_specs=(P(dp, "ep", None), P(dp, "ep")),
        check_vma=False,
    )
```

```python
import jax
import jax.numpy as jnp
from jax import lax
from jax.experimental import pallas as pl
from jax.experimental.pallas import tpu as pltpu
from jax.sharding import Mesh, PartitionSpec as P

LAT = 512
EXPERTS = 32
CAP = 8
PLANE = ("z", "y")
SOFTMAX_SCALE = 192 ** (-0.5)
BF = jnp.bfloat16
F32 = jnp.float32


def shifted(x, axis, by):
    devices = lax.axis_size(axis)
    return lax.ppermute(x, axis, [(i, (i + by) % devices) for i in range(devices)])


def attend(queries, latent_cache, lengths, core):
    span = latent_cache.shape[1]
    heads = queries.shape[1] // 2
    scores = jnp.einsum("shc,stc->sht", queries, latent_cache, preferred_element_type=F32)
    scores = scores * SOFTMAX_SCALE
    positions = core * span + jnp.arange(span, dtype=jnp.int32)
    valid = positions[None, None, :] < lengths[:, None, None]
    masked = jnp.where(valid, scores, -1e30)
    peak = jnp.max(masked, axis=2)
    weights = jnp.where(valid, jnp.exp(masked - peak[:, :, None]), 0.0)
    total = jnp.sum(weights, axis=2)
    numerator = jnp.einsum(
        "sht,stc->shc", weights.astype(BF), latent_cache[:, :, :LAT], preferred_element_type=F32
    )

    def mine(a):
        return lax.dynamic_slice_in_dim(a, core * heads, heads, 1)

    def other(a):
        return lax.dynamic_slice_in_dim(a, (1 - core) * heads, heads, 1)

    far_numerator = shifted(other(numerator).astype(BF), "ep", 1).astype(F32)
    far_stats = shifted(jnp.stack([other(peak), other(total)]), "ep", 1)
    near_peak, far_peak = mine(peak), far_stats[0]
    both = jnp.maximum(near_peak, far_peak)
    near_scale, far_scale = jnp.exp(near_peak - both), jnp.exp(far_peak - both)
    denominator = near_scale * mine(total) + far_scale * far_stats[1]
    combined = (
        near_scale[:, :, None] * mine(numerator) + far_scale[:, :, None] * far_numerator
    )
    return (combined / denominator[:, :, None]).astype(BF)


def slot_rows(core, hidden, norm_gain, routes, gate_weights):
    requests, model_width = hidden.shape
    half = model_width // 2
    slots = EXPERTS * CAP
    top = routes.shape[1]

    def kernel(core_ref, all_ref, half_ref, gain_ref, routes_ref, gates_ref, out_ref, mix_ref):
        del core_ref
        ids = routes_ref[...].astype(F32)
        gates = gates_ref[...].astype(F32)
        place = lax.broadcasted_iota(jnp.int32, (slots, requests), 0)
        expert = (place >> 3).astype(F32)
        member = jnp.zeros((slots, requests), F32)
        weight = jnp.zeros((slots, requests), F32)
        for k in range(top):
            hit = ids[k : k + 1, :] == expert
            member = jnp.where(hit, 1.0, member)
            weight = jnp.where(hit, gates[k : k + 1, :], weight)
        left = lax.broadcasted_iota(jnp.int32, (requests, requests), 0)
        right = lax.broadcasted_iota(jnp.int32, (requests, requests), 1)
        before = jnp.where(left < right, 1.0, 0.0).astype(BF)
        earlier = jnp.dot(member.astype(BF), before, preferred_element_type=F32)
        fits = (member > 0.5) & (earlier == (place & 7).astype(F32))
        mix_ref[...] = jnp.where(fits, weight, 0.0).astype(BF)
        chosen = jnp.where(fits, 1.0, 0.0).astype(BF)
        wide = all_ref[...].astype(F32)
        inverse = lax.rsqrt(jnp.mean(wide * wide, axis=1, keepdims=True) + 1e-06)
        for start in range(0, half, 512):
            columns = slice(start, start + 512)
            normed = half_ref[:, columns].astype(F32) * inverse * gain_ref[:, columns]
            out_ref[:, columns] = jnp.dot(
                chosen, normed.astype(BF), preferred_element_type=F32
            ).astype(BF)

    return pl.pallas_call(
        kernel,
        out_shape=(
            jax.ShapeDtypeStruct((slots, half), BF),
            jax.ShapeDtypeStruct((slots, requests), BF),
        ),
        grid_spec=pltpu.PrefetchScalarGridSpec(
            num_scalar_prefetch=1,
            grid=(1,),
            in_specs=[
                pl.BlockSpec((requests, model_width), lambda i, c: (0, 0)),
                pl.BlockSpec((requests, half), lambda i, c: (0, c[0])),
                pl.BlockSpec((1, half), lambda i, c: (0, c[0])),
                pl.BlockSpec((top, requests), lambda i, c: (0, 0)),
                pl.BlockSpec((top, requests), lambda i, c: (0, 0)),
            ],
            out_specs=(
                pl.BlockSpec((slots, half), lambda i, c: (0, 0)),
                pl.BlockSpec((slots, requests), lambda i, c: (0, 0)),
            ),
        ),
    )(core.reshape(1), hidden, hidden, norm_gain.reshape(1, -1), routes.T, gate_weights.T)


def add_experts(core, hidden, mix, returned):
    requests = hidden.shape[0]
    blocks, slots, width = returned.shape

    def kernel(core_ref, hidden_ref, mix_ref, returned_ref, out_ref):
        del core_ref
        weighted = lax.dot_general(
            mix_ref[...],
            returned_ref[0],
            (((0,), (0,)), ((), ())),
            preferred_element_type=F32,
        )
        out_ref[...] = (hidden_ref[...].astype(F32) + weighted).astype(BF)

    return pl.pallas_call(
        kernel,
        out_shape=jax.ShapeDtypeStruct((requests, blocks * width), BF),
        grid_spec=pltpu.PrefetchScalarGridSpec(
            num_scalar_prefetch=1,
            grid=(blocks,),
            in_specs=[
                pl.BlockSpec((requests, width), lambda i, c: (0, c[0] * blocks + i)),
                pl.BlockSpec((slots, requests), lambda i, c: (0, 0)),
                pl.BlockSpec((1, slots, width), lambda i, c: (i, 0, 0)),
            ],
            out_specs=pl.BlockSpec((requests, width), lambda i, c: (0, i)),
        ),
    )(core.reshape(1), hidden, mix, returned)


def local(
    queries,
    latent_cache,
    cache_lens,
    movers,
    hidden,
    norm_gain,
    routes,
    gate_weights,
    gate_proj,
    up_proj,
    down_proj,
):
    requests, model_width = hidden.shape
    half = model_width // 2
    count = EXPERTS * CAP
    core = lax.axis_index("ep").astype(jnp.int32)
    x_index = lax.axis_index("x").astype(jnp.int32)

    outbound, mix = slot_rows(core, hidden, norm_gain, routes, gate_weights)
    outbound, gate_proj, up_proj, down_proj = lax.optimization_barrier(
        (outbound, gate_proj, up_proj, down_proj)
    )
    rows = lax.all_to_all(
        outbound.reshape(EXPERTS, CAP, half), PLANE, split_axis=0, concat_axis=0, tiled=True
    ).reshape(count, half)

    both = jnp.concatenate([gate_proj[0], up_proj[0]], axis=1)
    far_weights = lax.dynamic_slice_in_dim(both, (1 - core) * half, half, 0)
    near_weights = lax.dynamic_slice_in_dim(both, core * half, half, 0)
    mixed = jnp.concatenate([near_weights, shifted(far_weights, "ep", 1)], axis=1)

    def down_rows(which):
        parts = []
        for by in range(4):
            source = (x_index + by) % 4
            parts.append(
                lax.dynamic_slice_in_dim(down_proj[0], source * 256 + which * 128, 128, 0)
            )
        return jnp.concatenate(parts, axis=0)

    near_down, far_down = down_rows(core), down_rows(1 - core)
    rows, mixed, near_down, far_down, queries, latent_cache, movers = (
        lax.optimization_barrier(
            (rows, mixed, near_down, far_down, queries, latent_cache, movers)
        )
    )

    ahead, behind = shifted(rows, "x", 1), shifted(rows, "x", -1)

    attention = attend(queries, latent_cache, cache_lens, core)
    listed = movers[0]
    slot_ids = jnp.arange(requests, dtype=jnp.int32)
    flagged = jnp.any(slot_ids[:, None] == listed[None, :], axis=1)
    nothing = jnp.zeros((), BF)
    picks = (listed[:, None] == slot_ids[None, :]).astype(BF)
    moved = jnp.einsum("mr,rhd->mhd", picks, attention, preferred_element_type=F32).astype(BF)
    arrived_contexts = shifted(moved, "z", 4)
    served = jnp.concatenate(
        [jnp.where(flagged[:, None, None], nothing, attention), arrived_contexts], axis=0
    )

    def products(blocks):
        return [jnp.dot(b, mixed, preferred_element_type=F32) for b in blocks]

    def activate(totals):
        total = jnp.concatenate(totals, axis=0)
        value = total[:, :256] + shifted(total[:, 256:], "ep", 1)
        activated = (jax.nn.silu(value[:, :128]) * value[:, 128:]).astype(BF)
        return activated.reshape(-1, count, 128)

    own = activate(products([rows]))
    ahead, behind, own, served = lax.optimization_barrier((ahead, behind, own, served))
    middle = count // 2
    across_low = shifted(ahead[:middle], "x", 1)
    across_high = shifted(behind[middle:], "x", -1)
    after_x, before_x = products([behind]), products([ahead])
    across_low, across_high, after_x, before_x = lax.optimization_barrier(
        (across_low, across_high, after_x, before_x)
    )
    others = activate(after_x + products([across_low, across_high]) + before_x)
    acts = jnp.concatenate([own, others], axis=0)
    held = [acts] + [shifted(acts, "x", -by) for by in (1, 2, 3)]
    stripes = [jnp.concatenate([held[s][(r - s) % 4] for s in range(4)], axis=1) for r in range(4)]
    twice = jnp.concatenate(stripes + stripes[:3], axis=0)
    joined = lax.dynamic_slice_in_dim(twice, (4 - x_index) % 4 * count, 4 * count, 0)
    expert_out = (
        jnp.dot(joined, near_down, preferred_element_type=F32)
        + jnp.dot(shifted(joined, "ep", 1), far_down, preferred_element_type=F32)
    ).astype(BF)
    returned = lax.all_to_all(
        expert_out.reshape(4 * EXPERTS, CAP, -1),
        ("x",) + PLANE,
        split_axis=0,
        concat_axis=0,
        tiled=True,
    )
    expert_mix = add_experts(core, hidden, mix, returned.reshape(4, count, -1))
    return served, expert_mix


def solution(mesh):
    grid = Mesh(mesh.devices.reshape(8, 4, 4, 2), ("z", "y", "x", "ep"))
    dp = ("z", "y", "x")
    placed = (
        P(dp, None, None),
        P(dp, "ep", None),
        P(dp),
        P(dp, None),
        P(dp, None),
        P(),
        P(dp, None),
        P(dp, None),
        P(dp, None, "ep"),
        P(dp, None, "ep"),
        P(dp, None, "ep"),
    )
    return jax.shard_map(
        local,
        mesh=grid,
        in_specs=placed,
        out_specs=(P(dp, "ep", None), P(dp, "ep")),
        check_vma=False,
    )
```

```python
import jax
import jax.numpy as jnp
from jax import lax
from jax.experimental import pallas as pl
from jax.experimental.pallas import tpu as pltpu
from jax.sharding import Mesh, PartitionSpec as P

LAT = 512
EXPERTS = 32
CAP = 8
PLANE = ("z", "y")
SOFTMAX_SCALE = 192 ** (-0.5)
BF = jnp.bfloat16
F32 = jnp.float32


def shifted(x, axis, by):
    devices = lax.axis_size(axis)
    return lax.ppermute(x, axis, [(i, (i + by) % devices) for i in range(devices)])


def attend(queries, latent_cache, lengths, core):
    span = latent_cache.shape[1]
    heads = queries.shape[1] // 2
    scores = jnp.einsum("shc,stc->sht", queries, latent_cache, preferred_element_type=F32)
    scores = scores * SOFTMAX_SCALE
    positions = core * span + jnp.arange(span, dtype=jnp.int32)
    valid = positions[None, None, :] < lengths[:, None, None]
    masked = jnp.where(valid, scores, -1e30)
    peak = jnp.max(masked, axis=2)
    weights = jnp.where(valid, jnp.exp(masked - peak[:, :, None]), 0.0)
    total = jnp.sum(weights, axis=2)
    numerator = jnp.einsum(
        "sht,stc->shc", weights.astype(BF), latent_cache[:, :, :LAT], preferred_element_type=F32
    )

    def mine(a):
        return lax.dynamic_slice_in_dim(a, core * heads, heads, 1)

    def other(a):
        return lax.dynamic_slice_in_dim(a, (1 - core) * heads, heads, 1)

    far_numerator = shifted(other(numerator).astype(BF), "ep", 1).astype(F32)
    far_stats = shifted(jnp.stack([other(peak), other(total)]), "ep", 1)
    near_peak, far_peak = mine(peak), far_stats[0]
    both = jnp.maximum(near_peak, far_peak)
    near_scale, far_scale = jnp.exp(near_peak - both), jnp.exp(far_peak - both)
    denominator = near_scale * mine(total) + far_scale * far_stats[1]
    combined = (
        near_scale[:, :, None] * mine(numerator) + far_scale[:, :, None] * far_numerator
    )
    return (combined / denominator[:, :, None]).astype(BF)


def slot_rows(core, hidden, norm_gain, routes, gate_weights):
    requests, model_width = hidden.shape
    half = model_width // 2
    slots = EXPERTS * CAP
    top = routes.shape[1]

    part = half // 2

    def kernel(core_ref, all_ref, half_ref, gain_ref, routes_ref, gates_ref, *out_refs):
        del core_ref
        ids = routes_ref[...].astype(F32)
        gates = gates_ref[...].astype(F32)
        place = lax.broadcasted_iota(jnp.int32, (slots, requests), 0)
        expert = (place >> 3).astype(F32)
        member = jnp.zeros((slots, requests), F32)
        weight = jnp.zeros((slots, requests), F32)
        for k in range(top):
            hit = ids[k : k + 1, :] == expert
            member = jnp.where(hit, 1.0, member)
            weight = jnp.where(hit, gates[k : k + 1, :], weight)
        left = lax.broadcasted_iota(jnp.int32, (requests, requests), 0)
        right = lax.broadcasted_iota(jnp.int32, (requests, requests), 1)
        before = jnp.where(left < right, 1.0, 0.0).astype(BF)
        earlier = jnp.dot(member.astype(BF), before, preferred_element_type=F32)
        fits = (member > 0.5) & (earlier == (place & 7).astype(F32))
        out_refs[2][...] = jnp.where(fits, weight, 0.0).astype(BF)
        chosen = jnp.where(fits, 1.0, 0.0).astype(BF)
        wide = all_ref[...].astype(F32)
        inverse = lax.rsqrt(jnp.mean(wide * wide, axis=1, keepdims=True) + 1e-06)
        for start in range(0, half, 256):
            columns = slice(start, start + 256)
            normed = half_ref[:, columns].astype(F32) * inverse * gain_ref[:, columns]
            out_refs[start // part][:, start % part : start % part + 256] = jnp.dot(
                chosen, normed.astype(BF), preferred_element_type=F32
            ).astype(BF)

    return pl.pallas_call(
        kernel,
        out_shape=(
            jax.ShapeDtypeStruct((slots, part), BF),
            jax.ShapeDtypeStruct((slots, part), BF),
            jax.ShapeDtypeStruct((slots, requests), BF),
        ),
        grid_spec=pltpu.PrefetchScalarGridSpec(
            num_scalar_prefetch=1,
            grid=(1,),
            in_specs=[
                pl.BlockSpec((requests, model_width), lambda i, c: (0, 0)),
                pl.BlockSpec((requests, half), lambda i, c: (0, c[0])),
                pl.BlockSpec((1, half), lambda i, c: (0, c[0])),
                pl.BlockSpec((top, requests), lambda i, c: (0, 0)),
                pl.BlockSpec((top, requests), lambda i, c: (0, 0)),
            ],
            out_specs=(
                pl.BlockSpec((slots, part), lambda i, c: (0, 0)),
                pl.BlockSpec((slots, part), lambda i, c: (0, 0)),
                pl.BlockSpec((slots, requests), lambda i, c: (0, 0)),
            ),
        ),
    )(core.reshape(1), hidden, hidden, norm_gain.reshape(1, -1), routes.T, gate_weights.T)


def add_experts(core, hidden, mix, returned):
    requests = hidden.shape[0]
    blocks, slots, width = returned.shape
    half = blocks * width

    def kernel(core_ref, hidden_ref, mix_ref, returned_ref, out_ref):
        own = hidden_ref[:, pl.ds(pl.multiple_of(core_ref[0] * half, 128), half)]
        for n in range(blocks):
            columns = slice(n * width, (n + 1) * width)
            weighted = lax.dot_general(
                mix_ref[...],
                returned_ref[n],
                (((0,), (0,)), ((), ())),
                preferred_element_type=F32,
            )
            out_ref[:, columns] = (own[:, columns].astype(F32) + weighted).astype(BF)

    vmem = pl.BlockSpec(memory_space=pltpu.VMEM)
    return pl.pallas_call(
        kernel,
        out_shape=jax.ShapeDtypeStruct((requests, half), BF),
        in_specs=[pl.BlockSpec(memory_space=pltpu.SMEM)] + [vmem] * 3,
        out_specs=vmem,
    )(core.reshape(1), hidden, mix, returned)


def local(
    queries,
    latent_cache,
    cache_lens,
    movers,
    hidden,
    norm_gain,
    routes,
    gate_weights,
    gate_proj,
    up_proj,
    down_proj,
):
    requests, model_width = hidden.shape
    half = model_width // 2
    count = EXPERTS * CAP
    core = lax.axis_index("ep").astype(jnp.int32)
    x_index = lax.axis_index("x").astype(jnp.int32)

    first, second, mix = slot_rows(core, hidden, norm_gain, routes, gate_weights)
    first, second, gate_proj, up_proj, down_proj = lax.optimization_barrier(
        (first, second, gate_proj, up_proj, down_proj)
    )

    def along_plane(part):
        part = part.reshape(EXPERTS, CAP, -1)
        part = lax.all_to_all(part, PLANE, split_axis=0, concat_axis=0, tiled=True)
        return part.reshape(count, -1)

    first = along_plane(first)
    first, second = lax.optimization_barrier((first, second))

    both = jnp.concatenate([gate_proj[0], up_proj[0]], axis=1)
    far_weights = lax.dynamic_slice_in_dim(both, (1 - core) * half, half, 0)
    near_weights = lax.dynamic_slice_in_dim(both, core * half, half, 0)
    mixed = jnp.concatenate([near_weights, shifted(far_weights, "ep", 1)], axis=1)

    def down_rows(which):
        parts = []
        for by in range(4):
            source = (x_index + by) % 4
            parts.append(
                lax.dynamic_slice_in_dim(down_proj[0], source * 256 + which * 128, 128, 0)
            )
        return jnp.concatenate(parts, axis=0)

    near_down, far_down = down_rows(core), down_rows(1 - core)
    gathered = lax.all_gather(first, "x", axis=0, tiled=True)
    second = along_plane(second)
    second, mixed, near_down, far_down, queries, latent_cache, movers = (
        lax.optimization_barrier(
            (second, mixed, near_down, far_down, queries, latent_cache, movers)
        )
    )
    ahead, behind = shifted(second, "x", 1), shifted(second, "x", -1)

    attention = attend(queries, latent_cache, cache_lens, core)
    listed = movers[0]
    slot_ids = jnp.arange(requests, dtype=jnp.int32)
    flagged = jnp.any(slot_ids[:, None] == listed[None, :], axis=1)
    nothing = jnp.zeros((), BF)
    picks = (listed[:, None] == slot_ids[None, :]).astype(BF)
    moved = jnp.einsum("mr,rhd->mhd", picks, attention, preferred_element_type=F32).astype(BF)
    arrived_contexts = shifted(moved, "z", 4)
    served = jnp.concatenate(
        [jnp.where(flagged[:, None, None], nothing, attention), arrived_contexts], axis=0
    )

    def product(rows, features):
        return jnp.dot(rows, mixed[features], preferred_element_type=F32)

    early, late = slice(0, half // 2), slice(half // 2, half)

    def activate(totals):
        total = jnp.concatenate(totals, axis=0)
        value = total[:, :256] + shifted(total[:, 256:], "ep", 1)
        activated = (jax.nn.silu(value[:, :128]) * value[:, 128:]).astype(BF)
        return activated.reshape(-1, count, 128)

    own = activate([product(first, early) + product(second, late)])
    ahead, behind, own = lax.optimization_barrier((ahead, behind, own))
    middle = count // 2
    across_low = shifted(ahead[:middle], "x", 1)
    across_high = shifted(behind[middle:], "x", -1)
    after_x, before_x = product(behind, late), product(ahead, late)
    across_low, across_high, after_x, before_x, served = lax.optimization_barrier(
        (across_low, across_high, after_x, before_x, served)
    )
    in_order = product(gathered, early)

    def early_part(by):
        return lax.dynamic_slice_in_dim(in_order, (x_index + by) % 4 * count, count, 0)

    opposite = jnp.concatenate([product(across_low, late), product(across_high, late)], axis=0)
    others = activate(
        [early_part(1) + after_x, early_part(2) + opposite, early_part(3) + before_x]
    )
    acts = jnp.concatenate([own, others], axis=0)
    held = [acts] + [shifted(acts, "x", -by) for by in (1, 2, 3)]
    stripes = [jnp.concatenate([held[s][(r - s) % 4] for s in range(4)], axis=1) for r in range(4)]
    twice = jnp.concatenate(stripes + stripes[:3], axis=0)
    joined = lax.dynamic_slice_in_dim(twice, (4 - x_index) % 4 * count, 4 * count, 0)
    expert_out = (
        jnp.dot(joined, near_down, preferred_element_type=F32)
        + jnp.dot(shifted(joined, "ep", 1), far_down, preferred_element_type=F32)
    ).astype(BF)
    returned = lax.all_to_all(
        expert_out.reshape(4 * EXPERTS, CAP, -1),
        ("x",) + PLANE,
        split_axis=0,
        concat_axis=0,
        tiled=True,
    )
    expert_mix = add_experts(core, hidden, mix, returned.reshape(4, count, -1))
    return served, expert_mix


def solution(mesh):
    grid = Mesh(mesh.devices.reshape(8, 4, 4, 2), ("z", "y", "x", "ep"))
    dp = ("z", "y", "x")
    placed = (
        P(dp, None, None),
        P(dp, "ep", None),
        P(dp),
        P(dp, None),
        P(dp, None),
        P(),
        P(dp, None),
        P(dp, None),
        P(dp, None, "ep"),
        P(dp, None, "ep"),
        P(dp, None, "ep"),
    )
    return jax.shard_map(
        local,
        mesh=grid,
        in_specs=placed,
        out_specs=(P(dp, "ep", None), P(dp, "ep")),
        check_vma=False,
    )
```

```python
import jax
import jax.numpy as jnp
from jax import lax
from jax.experimental import pallas as pl
from jax.experimental.pallas import tpu as pltpu
from jax.sharding import Mesh, PartitionSpec as P

LAT = 512
EXPERTS = 32
CAP = 8
PLANE = ("z", "y")
SOFTMAX_SCALE = 192 ** (-0.5)
BF = jnp.bfloat16
F32 = jnp.float32


def shifted(x, axis, by):
    devices = lax.axis_size(axis)
    return lax.ppermute(x, axis, [(i, (i + by) % devices) for i in range(devices)])


def attend(queries, latent_cache, lengths, core):
    span = latent_cache.shape[1]
    heads = queries.shape[1] // 2
    scores = jnp.einsum("shc,stc->sht", queries, latent_cache, preferred_element_type=F32)
    scores = scores * SOFTMAX_SCALE
    positions = core * span + jnp.arange(span, dtype=jnp.int32)
    valid = positions[None, None, :] < lengths[:, None, None]
    masked = jnp.where(valid, scores, -1e30)
    peak = jnp.max(masked, axis=2)
    weights = jnp.where(valid, jnp.exp(masked - peak[:, :, None]), 0.0)
    total = jnp.sum(weights, axis=2)
    numerator = jnp.einsum(
        "sht,stc->shc", weights.astype(BF), latent_cache[:, :, :LAT], preferred_element_type=F32
    )

    def mine(a):
        return lax.dynamic_slice_in_dim(a, core * heads, heads, 1)

    def other(a):
        return lax.dynamic_slice_in_dim(a, (1 - core) * heads, heads, 1)

    far_numerator = shifted(other(numerator).astype(BF), "ep", 1).astype(F32)
    far_stats = shifted(jnp.stack([other(peak), other(total)]), "ep", 1)
    near_peak, far_peak = mine(peak), far_stats[0]
    both = jnp.maximum(near_peak, far_peak)
    near_scale, far_scale = jnp.exp(near_peak - both), jnp.exp(far_peak - both)
    denominator = near_scale * mine(total) + far_scale * far_stats[1]
    combined = (
        near_scale[:, :, None] * mine(numerator) + far_scale[:, :, None] * far_numerator
    )
    return (combined / denominator[:, :, None]).astype(BF)


def slot_rows(core, hidden, norm_gain, routes, gate_weights):
    requests, model_width = hidden.shape
    half = model_width // 2
    slots = EXPERTS * CAP
    top = routes.shape[1]
    width = half // 4

    def kernel(core_ref, all_ref, half_ref, gain_ref, routes_ref, gates_ref, out_ref, mix_ref):
        del core_ref
        ids = routes_ref[...].astype(F32)
        gates = gates_ref[...].astype(F32)
        place = lax.broadcasted_iota(jnp.int32, (slots, requests), 0)
        expert = (place >> 3).astype(F32)
        member = jnp.zeros((slots, requests), F32)
        weight = jnp.zeros((slots, requests), F32)
        for k in range(top):
            hit = ids[k : k + 1, :] == expert
            member = jnp.where(hit, 1.0, member)
            weight = jnp.where(hit, gates[k : k + 1, :], weight)
        left = lax.broadcasted_iota(jnp.int32, (requests, requests), 0)
        right = lax.broadcasted_iota(jnp.int32, (requests, requests), 1)
        before = jnp.where(left < right, 1.0, 0.0).astype(BF)
        earlier = jnp.dot(member.astype(BF), before, preferred_element_type=F32)
        fits = (member > 0.5) & (earlier == (place & 7).astype(F32))
        mix_ref[...] = jnp.where(fits, weight, 0.0).astype(BF)
        chosen = jnp.where(fits, 1.0, 0.0).astype(BF)
        wide = all_ref[...].astype(F32)
        inverse = lax.rsqrt(jnp.mean(wide * wide, axis=1, keepdims=True) + 1e-06)
        for n in range(4):
            columns = slice(n * width, (n + 1) * width)
            normed = half_ref[:, columns].astype(F32) * inverse * gain_ref[:, columns]
            out_ref[n] = jnp.dot(
                chosen, normed.astype(BF), preferred_element_type=F32
            ).astype(BF)

    return pl.pallas_call(
        kernel,
        out_shape=(
            jax.ShapeDtypeStruct((4, slots, width), BF),
            jax.ShapeDtypeStruct((slots, requests), BF),
        ),
        grid_spec=pltpu.PrefetchScalarGridSpec(
            num_scalar_prefetch=1,
            grid=(1,),
            in_specs=[
                pl.BlockSpec((requests, model_width), lambda i, c: (0, 0)),
                pl.BlockSpec((requests, half), lambda i, c: (0, c[0])),
                pl.BlockSpec((1, half), lambda i, c: (0, c[0])),
                pl.BlockSpec((top, requests), lambda i, c: (0, 0)),
                pl.BlockSpec((top, requests), lambda i, c: (0, 0)),
            ],
            out_specs=(
                pl.BlockSpec((4, slots, width), lambda i, c: (0, 0, 0)),
                pl.BlockSpec((slots, requests), lambda i, c: (0, 0)),
            ),
        ),
    )(core.reshape(1), hidden, hidden, norm_gain.reshape(1, -1), routes.T, gate_weights.T)


def add_experts(core, hidden, mix, returned):
    requests = hidden.shape[0]
    blocks, slots, width = returned.shape
    half = blocks * width

    def kernel(core_ref, hidden_ref, mix_ref, returned_ref, out_ref):
        own = hidden_ref[:, pl.ds(pl.multiple_of(core_ref[0] * half, 128), half)]
        for n in range(blocks):
            columns = slice(n * width, (n + 1) * width)
            weighted = lax.dot_general(
                mix_ref[...],
                returned_ref[n],
                (((0,), (0,)), ((), ())),
                preferred_element_type=F32,
            )
            out_ref[:, columns] = (own[:, columns].astype(F32) + weighted).astype(BF)

    vmem = pl.BlockSpec(memory_space=pltpu.VMEM)
    return pl.pallas_call(
        kernel,
        out_shape=jax.ShapeDtypeStruct((requests, half), BF),
        in_specs=[pl.BlockSpec(memory_space=pltpu.SMEM)] + [vmem] * 3,
        out_specs=vmem,
    )(core.reshape(1), hidden, mix, returned)


def local(
    queries,
    latent_cache,
    cache_lens,
    movers,
    hidden,
    norm_gain,
    routes,
    gate_weights,
    gate_proj,
    up_proj,
    down_proj,
):
    requests, model_width = hidden.shape
    half = model_width // 2
    count = EXPERTS * CAP
    core = lax.axis_index("ep").astype(jnp.int32)
    x_index = lax.axis_index("x").astype(jnp.int32)

    outbound, mix = slot_rows(core, hidden, norm_gain, routes, gate_weights)
    outbound, gate_proj, up_proj, down_proj = lax.optimization_barrier(
        (outbound, gate_proj, up_proj, down_proj)
    )
    rows = lax.all_to_all(
        outbound.reshape(4 * EXPERTS, CAP, -1),
        ("x",) + PLANE,
        split_axis=0,
        concat_axis=0,
        tiled=True,
    ).reshape(4 * count, -1)

    both = jnp.concatenate([gate_proj[0], up_proj[0]], axis=1)
    far_weights = lax.dynamic_slice_in_dim(both, (1 - core) * half, half, 0)
    near_weights = lax.dynamic_slice_in_dim(both, core * half, half, 0)
    mixed = jnp.concatenate([near_weights, shifted(far_weights, "ep", 1)], axis=1)

    quarter = half // 4

    def features_of(by):
        return lax.dynamic_slice_in_dim(mixed, (x_index + 4 - by) % 4 * quarter, quarter, 0)

    weights = [features_of(0)] + [shifted(features_of(by), "x", -by) for by in (1, 2, 3)]

    def down_rows(which):
        parts = []
        for by in range(4):
            source = (x_index + by) % 4
            parts.append(
                lax.dynamic_slice_in_dim(down_proj[0], source * 256 + which * 128, 128, 0)
            )
        return jnp.concatenate(parts, axis=0)

    near_down, far_down = down_rows(core), down_rows(1 - core)
    rows, weights, near_down, far_down, queries, latent_cache, movers = (
        lax.optimization_barrier(
            (rows, weights, near_down, far_down, queries, latent_cache, movers)
        )
    )

    partial = [jnp.dot(rows, w, preferred_element_type=F32) for w in weights]
    other_core = shifted(jnp.concatenate([p[:, 256:].astype(BF) for p in partial], axis=1), "ep", 1)
    sums = [
        p[:, :256] + other_core[:, n * 256 : (n + 1) * 256].astype(F32)
        for n, p in enumerate(partial)
    ]
    arrived = [shifted(sums[by].astype(BF), "x", by) for by in (1, 2, 3)]

    attention = attend(queries, latent_cache, cache_lens, core)
    listed = movers[0]
    slot_ids = jnp.arange(requests, dtype=jnp.int32)
    flagged = jnp.any(slot_ids[:, None] == listed[None, :], axis=1)
    nothing = jnp.zeros((), BF)
    picks = (listed[:, None] == slot_ids[None, :]).astype(BF)
    moved = jnp.einsum("mr,rhd->mhd", picks, attention, preferred_element_type=F32).astype(BF)
    arrived_contexts = shifted(moved, "z", 4)
    served = jnp.concatenate(
        [jnp.where(flagged[:, None, None], nothing, attention), arrived_contexts], axis=0
    )

    value = sums[0] + sum(part.astype(F32) for part in arrived)
    acts = (jax.nn.silu(value[:, :128]) * value[:, 128:]).astype(BF)
    acts, served = lax.optimization_barrier((acts, served))
    held = [acts] + [shifted(acts, "x", -by) for by in (1, 2, 3)]
    joined = jnp.concatenate(held, axis=1)
    expert_out = (
        jnp.dot(joined, near_down, preferred_element_type=F32)
        + jnp.dot(shifted(joined, "ep", 1), far_down, preferred_element_type=F32)
    ).astype(BF)
    returned = lax.all_to_all(
        expert_out.reshape(4 * EXPERTS, CAP, -1),
        ("x",) + PLANE,
        split_axis=0,
        concat_axis=0,
        tiled=True,
    )
    expert_mix = add_experts(core, hidden, mix, returned.reshape(4, count, -1))
    return served, expert_mix


def solution(mesh):
    grid = Mesh(mesh.devices.reshape(8, 4, 4, 2), ("z", "y", "x", "ep"))
    dp = ("z", "y", "x")
    placed = (
        P(dp, None, None),
        P(dp, "ep", None),
        P(dp),
        P(dp, None),
        P(dp, None),
        P(),
        P(dp, None),
        P(dp, None),
        P(dp, None, "ep"),
        P(dp, None, "ep"),
        P(dp, None, "ep"),
    )
    return jax.shard_map(
        local,
        mesh=grid,
        in_specs=placed,
        out_specs=(P(dp, "ep", None), P(dp, "ep")),
        check_vma=False,
    )
```

```python
import jax
import jax.numpy as jnp
from jax import lax
from jax.experimental import pallas as pl
from jax.experimental.pallas import tpu as pltpu
from jax.sharding import Mesh, PartitionSpec as P

LAT = 512
EXPERTS = 32
CAP = 8
PLANE = ("z", "y")
SOFTMAX_SCALE = 192 ** (-0.5)
BF = jnp.bfloat16
F32 = jnp.float32


def shifted(x, axis, by):
    devices = lax.axis_size(axis)
    return lax.ppermute(x, axis, [(i, (i + by) % devices) for i in range(devices)])


def attend(queries, latent_cache, lengths, core):
    span = latent_cache.shape[1]
    heads = queries.shape[1] // 2
    scores = jnp.einsum("shc,stc->sht", queries, latent_cache, preferred_element_type=F32)
    scores = scores * SOFTMAX_SCALE
    positions = core * span + jnp.arange(span, dtype=jnp.int32)
    valid = positions[None, None, :] < lengths[:, None, None]
    masked = jnp.where(valid, scores, -1e30)
    peak = jnp.max(masked, axis=2)
    weights = jnp.where(valid, jnp.exp(masked - peak[:, :, None]), 0.0)
    total = jnp.sum(weights, axis=2)
    numerator = jnp.einsum(
        "sht,stc->shc", weights.astype(BF), latent_cache[:, :, :LAT], preferred_element_type=F32
    )

    def mine(a):
        return lax.dynamic_slice_in_dim(a, core * heads, heads, 1)

    def other(a):
        return lax.dynamic_slice_in_dim(a, (1 - core) * heads, heads, 1)

    far_numerator = shifted(other(numerator).astype(BF), "ep", 1).astype(F32)
    far_stats = shifted(jnp.stack([other(peak), other(total)]), "ep", 1)
    near_peak, far_peak = mine(peak), far_stats[0]
    both = jnp.maximum(near_peak, far_peak)
    near_scale, far_scale = jnp.exp(near_peak - both), jnp.exp(far_peak - both)
    denominator = near_scale * mine(total) + far_scale * far_stats[1]
    combined = (
        near_scale[:, :, None] * mine(numerator) + far_scale[:, :, None] * far_numerator
    )
    return (combined / denominator[:, :, None]).astype(BF)


def slot_rows(core, hidden, norm_gain, routes, gate_weights):
    requests, model_width = hidden.shape
    half = model_width // 2
    slots = EXPERTS * CAP
    top = routes.shape[1]

    def kernel(core_ref, all_ref, gain_ref, routes_ref, gates_ref, out_ref, mix_ref):
        base = core_ref[0] * half
        ids = routes_ref[...].astype(F32)
        gates = gates_ref[...].astype(F32)
        place = lax.broadcasted_iota(jnp.int32, (slots, requests), 0)
        expert = (place >> 3).astype(F32)
        member = jnp.zeros((slots, requests), F32)
        weight = jnp.zeros((slots, requests), F32)
        for k in range(top):
            hit = ids[k : k + 1, :] == expert
            member = jnp.where(hit, 1.0, member)
            weight = jnp.where(hit, gates[k : k + 1, :], weight)
        left = lax.broadcasted_iota(jnp.int32, (requests, requests), 0)
        right = lax.broadcasted_iota(jnp.int32, (requests, requests), 1)
        before = jnp.where(left < right, 1.0, 0.0).astype(BF)
        earlier = jnp.dot(member.astype(BF), before, preferred_element_type=F32)
        fits = (member > 0.5) & (earlier == (place & 7).astype(F32))
        mix_ref[...] = jnp.where(fits, weight, 0.0).astype(BF)
        chosen = jnp.where(fits, 1.0, 0.0).astype(BF)
        wide = all_ref[...].astype(F32)
        inverse = lax.rsqrt(jnp.mean(wide * wide, axis=1, keepdims=True) + 1e-06)
        for start in range(0, half, 512):
            columns = slice(start, start + 512)
            own = pl.ds(pl.multiple_of(base + start, 128), 512)
            normed = all_ref[:, own].astype(F32) * inverse * gain_ref[:, own]
            out_ref[:, columns] = jnp.dot(
                chosen, normed.astype(BF), preferred_element_type=F32
            ).astype(BF)

    vmem = pl.BlockSpec(memory_space=pltpu.VMEM)
    return pl.pallas_call(
        kernel,
        out_shape=(
            jax.ShapeDtypeStruct((slots, half), BF),
            jax.ShapeDtypeStruct((slots, requests), BF),
        ),
        in_specs=[pl.BlockSpec(memory_space=pltpu.SMEM)] + [vmem] * 4,
        out_specs=(vmem, vmem),
    )(core.reshape(1), hidden, norm_gain.reshape(1, -1), routes.T, gate_weights.T)


def add_experts(core, hidden, mix, returned):
    requests = hidden.shape[0]
    blocks, slots, width = returned.shape
    half = blocks * width

    def kernel(core_ref, hidden_ref, mix_ref, returned_ref, out_ref):
        own = hidden_ref[:, pl.ds(pl.multiple_of(core_ref[0] * half, 128), half)]
        for n in range(blocks):
            columns = slice(n * width, (n + 1) * width)
            weighted = lax.dot_general(
                mix_ref[...],
                returned_ref[n],
                (((0,), (0,)), ((), ())),
                preferred_element_type=F32,
            )
            out_ref[:, columns] = (own[:, columns].astype(F32) + weighted).astype(BF)

    vmem = pl.BlockSpec(memory_space=pltpu.VMEM)
    return pl.pallas_call(
        kernel,
        out_shape=jax.ShapeDtypeStruct((requests, half), BF),
        in_specs=[pl.BlockSpec(memory_space=pltpu.SMEM)] + [vmem] * 3,
        out_specs=vmem,
    )(core.reshape(1), hidden, mix, returned)


def local(
    queries,
    latent_cache,
    cache_lens,
    movers,
    hidden,
    norm_gain,
    routes,
    gate_weights,
    gate_proj,
    up_proj,
    down_proj,
):
    requests, model_width = hidden.shape
    half = model_width // 2
    count = EXPERTS * CAP
    core = lax.axis_index("ep").astype(jnp.int32)
    x_index = lax.axis_index("x").astype(jnp.int32)

    outbound, mix = slot_rows(core, hidden, norm_gain, routes, gate_weights)
    outbound, gate_proj, up_proj, down_proj = lax.optimization_barrier(
        (outbound, gate_proj, up_proj, down_proj)
    )
    rows = lax.all_to_all(
        outbound.reshape(EXPERTS, CAP, half), PLANE, split_axis=0, concat_axis=0, tiled=True
    ).reshape(count, half)

    both = jnp.concatenate([gate_proj[0], up_proj[0]], axis=1)
    far_weights = lax.dynamic_slice_in_dim(both, (1 - core) * half, half, 0)
    near_weights = lax.dynamic_slice_in_dim(both, core * half, half, 0)
    mixed = jnp.concatenate([near_weights, shifted(far_weights, "ep", 1)], axis=1)

    def down_rows(which):
        parts = []
        for by in range(4):
            source = (x_index + by) % 4
            parts.append(
                lax.dynamic_slice_in_dim(down_proj[0], source * 256 + which * 128, 128, 0)
            )
        return jnp.concatenate(parts, axis=0)

    near_down, far_down = down_rows(core), down_rows(1 - core)
    rows, mixed, near_down, far_down, queries, latent_cache, movers = (
        lax.optimization_barrier(
            (rows, mixed, near_down, far_down, queries, latent_cache, movers)
        )
    )

    ahead, behind = shifted(rows, "x", 1), shifted(rows, "x", -1)

    attention = attend(queries, latent_cache, cache_lens, core)
    listed = movers[0]
    slot_ids = jnp.arange(requests, dtype=jnp.int32)
    flagged = jnp.any(slot_ids[:, None] == listed[None, :], axis=1)
    nothing = jnp.zeros((), BF)
    picks = (listed[:, None] == slot_ids[None, :]).astype(BF)
    moved = jnp.einsum("mr,rhd->mhd", picks, attention, preferred_element_type=F32).astype(BF)
    arrived_contexts = shifted(moved, "z", 4)
    served = jnp.concatenate(
        [jnp.where(flagged[:, None, None], nothing, attention), arrived_contexts], axis=0
    )

    def products(blocks):
        return [jnp.dot(b, mixed, preferred_element_type=F32) for b in blocks]

    def activate(totals):
        total = jnp.concatenate(totals, axis=0)
        value = total[:, :256] + shifted(total[:, 256:], "ep", 1)
        activated = (jax.nn.silu(value[:, :128]) * value[:, 128:]).astype(BF)
        return activated.reshape(-1, count, 128)

    own = activate(products([rows]))
    ahead, behind, own, served = lax.optimization_barrier((ahead, behind, own, served))
    middle = count // 2
    across_low = shifted(ahead[:middle], "x", 1)
    across_high = shifted(behind[middle:], "x", -1)
    after_x, before_x = products([behind]), products([ahead])
    across_low, across_high, after_x, before_x = lax.optimization_barrier(
        (across_low, across_high, after_x, before_x)
    )
    others = activate(after_x + products([across_low, across_high]) + before_x)
    acts = jnp.concatenate([own, others], axis=0)
    held = [acts] + [shifted(acts, "x", -by) for by in (1, 2, 3)]
    stripes = [jnp.concatenate([held[s][(r - s) % 4] for s in range(4)], axis=1) for r in range(4)]
    twice = jnp.concatenate(stripes + stripes[:3], axis=0)
    joined = lax.dynamic_slice_in_dim(twice, (4 - x_index) % 4 * count, 4 * count, 0)
    expert_out = (
        jnp.dot(joined, near_down, preferred_element_type=F32)
        + jnp.dot(shifted(joined, "ep", 1), far_down, preferred_element_type=F32)
    ).astype(BF)
    returned = lax.all_to_all(
        expert_out.reshape(4 * EXPERTS, CAP, -1),
        ("x",) + PLANE,
        split_axis=0,
        concat_axis=0,
        tiled=True,
    )
    expert_mix = add_experts(core, hidden, mix, returned.reshape(4, count, -1))
    return served, expert_mix


def solution(mesh):
    grid = Mesh(mesh.devices.reshape(8, 4, 4, 2), ("z", "y", "x", "ep"))
    dp = ("z", "y", "x")
    placed = (
        P(dp, None, None),
        P(dp, "ep", None),
        P(dp),
        P(dp, None),
        P(dp, None),
        P(),
        P(dp, None),
        P(dp, None),
        P(dp, None, "ep"),
        P(dp, None, "ep"),
        P(dp, None, "ep"),
    )
    return jax.shard_map(
        local,
        mesh=grid,
        in_specs=placed,
        out_specs=(P(dp, "ep", None), P(dp, "ep")),
        check_vma=False,
    )
```
